32 devices in a mesh: slide: 4 (over x, core), tile: 8 (over z, y).
Axes of the slice: x: 2, y: 2, z: 4, core: 2. Of those that a mesh axis runs over, the one named last changes fastest.
Arguments:
- features: bfloat16 [4, 512, 16, 16, 128], P('slide', 'tile'), may hold values from -6 to 6
- tissue_count: int32 [4, 8], P('slide', 'tile'), may hold values from 0 to 64, as said below
- neighbors: int32 [4, 512, 8], P('slide', 'tile'), may hold values from -1 to 511, as said below
- worker_perm: int32 [4, 8], P('slide'), may hold values from 0 to 7, each once within a row
- rotation: int32 [4], P('slide'), may hold values from 0 to 255
- kernel: bfloat16 [9, 128], replicated, may hold values from -2 to 2
- gain: float32 [128], replicated, may hold values from 0.1 to 1.9
- w_in: bfloat16 [128, 512], replicated, may hold values from -0.5 to 0.5
- w_out: bfloat16 [512, 128], replicated, may hold values from -0.25 to 0.25
- cotangent: float32 [4, 256, 128], P('slide', 'tile'), may hold values from -0.3 to 0.3
Outputs:
- embed: float32 [4, 256, 128], P('slide', 'tile')
- grad_kernel: float32 [9, 128], replicated
- grad_gain: float32 [128], replicated
- grad_in: float32 [128, 512], replicated
- grad_out: float32 [512, 128], replicated
The draws below stay inside these ranges and needn't reach their ends.
Inputs may be any that keep to these rules, and one draw needn't show every extreme that they name: `tissue_count`: in each group the counts sum to 256. `neighbors`: each entry is -1 or the slot number q * 64 + j of a tissue slot (j below tissue_count of q) of an owner q equal to the slot's own owner or next to it in the same group; slots at or past their owner's count have -1 everywhere.
All inputs are finite; a program needn't handle non-finite values.
Results may differ from the reference program's by a relative error of at most 0.00065.
Values may be sent and summed in bfloat16 or wider, within the bound.
No kernel may reach another device: no remote copies, remote signals or barrier semaphores. Data moves between devices by JAX's collectives and lax.ppermute only.
A program may use at most 64 MiB of HBM per device.

```python
import math
import jax
import jax.numpy as jnp
from jax import lax

C = 128
HID = 512
P_SIZE = 16
WORK_DEV = 32
TILES_DEV = 64
GROUPS = 4
SLOTS = 512
WORKS = 256
N_TILE = 8


def counts_helper(key):
    keys = jax.random.split(jax.random.fold_in(key, 11), GROUPS)

    def one_group(group_key):
        first_key, second_key, third_key = jax.random.split(group_key, 3)
        half = N_TILE // 2
        spread = jax.random.randint(first_key, (half,), -WORK_DEV, WORK_DEV + 1)
        forced = jax.random.randint(second_key, (), 0, half)
        spread = jnp.where(jnp.arange(half) == forced, WORK_DEV, spread)
        paired = jnp.concatenate([WORK_DEV + spread, WORK_DEV - spread])
        return jax.random.permutation(third_key, paired)
    return jax.vmap(one_group)(keys).astype(jnp.int32)


def draw_tissue_count(key, part):
    return counts_helper(key)


def draw_neighbors(key, part):
    counts = counts_helper(key)
    first_key, second_key, third_key = jax.random.split(jax.random.fold_in(key, 23), 3)
    shape = (GROUPS, N_TILE, TILES_DEV, 8)
    offset = jax.random.randint(first_key, shape, -1, 2)
    owner = jnp.arange(N_TILE)[None, :, None, None] + offset
    inside = (owner >= 0) & (owner < N_TILE)
    safe_owner = jnp.clip(owner, 0, N_TILE - 1)
    theirs = jax.vmap(lambda table, where_at: table[where_at])(counts, safe_owner)
    chosen = jax.random.randint(second_key, shape, 0, 1048576) % jnp.maximum(theirs, 1)
    keep = jax.random.randint(third_key, shape, 0, 4) > 0
    mine = jnp.arange(TILES_DEV)[None, None, :, None] < counts[:, :, None, None]
    usable = inside & (theirs > 0) & keep & mine
    result = jnp.where(usable, safe_owner * TILES_DEV + chosen, -1)
    return result.reshape(GROUPS, SLOTS, 8).astype(jnp.int32)


def draw_features(key, part):
    first_key, second_key = jax.random.split(jax.random.fold_in(key, 37), 2)
    shape = (GROUPS, SLOTS, P_SIZE, P_SIZE, C)
    means = 0.8 * jax.random.normal(first_key, (GROUPS, SLOTS, 1, 1, C), jnp.float32)
    rough = jax.random.normal(second_key, shape, jnp.float32)
    return jnp.clip(means + rough, -6.0, 6.0).astype(jnp.bfloat16)


def set_ends(entries, rng, least, top_value):
    index_at = [jax.random.randint(jax.random.fold_in(rng, axis), (), 0, length) for axis, length in enumerate(entries.shape)]
    main_axis = entries.shape.index(max(entries.shape))
    next_to = index_at[:main_axis] + [(index_at[main_axis] + 1) % entries.shape[main_axis]] + index_at[main_axis + 1:]
    return entries.at[tuple(index_at)].set(least).at[tuple(next_to)].set(top_value)


def block_scale(rng, extent, cuts, low, high):
    def one(dim, blocks):
        draws = jax.random.uniform(jax.random.fold_in(jax.random.fold_in(rng, 6), dim), (blocks,), jnp.float32, low / len(cuts), high / len(cuts))
        return jnp.repeat(jnp.exp(draws), extent[dim] // blocks).reshape((-1,) + (1,) * (len(extent) - dim - 1))

    factor_of = one(*cuts[0])
    for cut in cuts[1:]:
        factor_of = factor_of * one(*cut)
    return factor_of


def normal_values(rng, extent, deviation, most, shards=(), kind=jnp.bfloat16):
    values = jax.random.normal(rng, extent, jnp.float32) * deviation
    if len(shards) > 0:
        values = block_scale(rng, extent, shards, -0.22, 0.18) * values
    return jnp.clip(values, min=-most, max=most).astype(kind)


def setup_inputs(seed: int = 0) -> dict:
    key_of = jax.random.split(jax.random.key(seed), 11)
    return {
        "features": draw_features(jax.random.fold_in(key_of[10], 71), 0),
        "tissue_count": draw_tissue_count(jax.random.fold_in(key_of[10], 71), 0),
        "neighbors": draw_neighbors(jax.random.fold_in(key_of[10], 71), 0),
        "worker_perm": jax.vmap(lambda own: jax.random.permutation(own, N_TILE))(jax.random.split(key_of[3], GROUPS)).reshape((GROUPS, N_TILE)).astype(jnp.int32),
        "rotation": set_ends(jax.random.randint(key_of[4], (GROUPS,), 0, WORKS), jax.random.fold_in(key_of[4], 1), 0, WORKS - 1).astype(jnp.int32),
        "kernel": normal_values(key_of[5], (9, C), 9 ** -0.5, 2.0),
        "gain": jnp.clip(1.0 + 0.18 * jax.random.normal(key_of[6], (C,), jnp.float32), 0.1, 1.9),
        "w_in": normal_values(key_of[7], (C, HID), C ** -0.5, 0.5),
        "w_out": normal_values(key_of[8], (HID, C), HID ** -0.5, 0.25),
        "cotangent": normal_values(key_of[9], (GROUPS, WORKS, C), 0.05, 0.3, ((0, 4), (1, 8)), jnp.float32),
    }


def border_rows(tiles):
    return jnp.stack([tiles[:, 0], tiles[:, -1], tiles[:, :, 0], tiles[:, :, -1]], axis=1)

def assemble(center, borders, index):
    side = center.shape[1]

    def pick(column, which):
        chosen = index[:, column]
        rows = jnp.take(borders[:, which], jnp.maximum(chosen, 0), axis=0)
        return jnp.where((chosen >= 0)[:, None, None], rows, jnp.zeros_like(rows))
    upper = pick(0, 1)
    lower = pick(1, 0)
    left_col = pick(2, 3)
    right_col = pick(3, 2)
    upper_left = pick(4, 1)[:, side - 1]
    upper_right = pick(5, 1)[:, 0]
    lower_left = pick(6, 0)[:, side - 1]
    lower_right = pick(7, 0)[:, 0]
    top = jnp.concatenate([upper_left[:, None], upper, upper_right[:, None]], axis=1)
    bottom = jnp.concatenate([lower_left[:, None], lower, lower_right[:, None]], axis=1)
    middle = jnp.concatenate([left_col[:, :, None], center, right_col[:, :, None]], axis=2)
    return jnp.concatenate([top[:, None], middle, bottom[:, None]], axis=1)

def gelu_value(before):
    return 0.5 * before * (1.0 + lax.erf(before * 0.7071067811865476))

def gelu_slope(before):
    return 0.5 * (1.0 + lax.erf(before * 0.7071067811865476)) + before * jnp.exp(-0.5 * before * before) * 0.3989422804014327

def block_section(padded, cot_rows, kernel, gain, w_in, w_out):
    count = padded.shape[0]
    side = padded.shape[1] - 2
    chans = padded.shape[3]
    pixels = side * side
    kernel_wide = kernel.astype(jnp.float32)
    shifted = [padded[:, row:row + side, col:col + side, :] for row in range(3) for col in range(3)]
    depth = shifted[0].astype(jnp.float32) * kernel_wide[0]
    for offset in range(1, 9):
        depth = depth + shifted[offset].astype(jnp.float32) * kernel_wide[offset]
    depth = depth.reshape(count * pixels, chans)
    channel_mean = lax.optimization_barrier(jnp.mean(depth, axis=1, keepdims=True))
    centered = depth - channel_mean
    inverse = lax.rsqrt(lax.optimization_barrier(jnp.mean(centered * centered, axis=1, keepdims=True)) + 1e-06)
    unit_values = centered * inverse
    normed = (unit_values * gain).astype(jnp.bfloat16)
    before = jnp.dot(normed, w_in, preferred_element_type=jnp.float32)
    hidden = before.shape[1]
    activated = gelu_value(before).astype(jnp.bfloat16)
    projected = jnp.dot(activated, w_out, preferred_element_type=jnp.float32)
    center = padded[:, 1:side + 1, 1:side + 1, :].astype(jnp.float32).reshape(count * pixels, chans)
    embed = lax.optimization_barrier(jnp.mean((center + projected).reshape(count, pixels, chans), axis=1))
    grad_embed = cot_rows / pixels
    act_sum = lax.optimization_barrier(jnp.sum(activated.reshape(count, pixels, hidden).astype(jnp.float32), axis=1))
    grad_out = jnp.dot(act_sum.T, grad_embed, precision=lax.Precision.HIGHEST)
    grad_act = jnp.dot(grad_embed, w_out.astype(jnp.float32).T, precision=lax.Precision.HIGHEST)
    grad_before = (grad_act[:, None, :] * gelu_slope(before).reshape(count, pixels, hidden)).astype(jnp.bfloat16)
    grad_before = grad_before.reshape(count * pixels, hidden)
    grad_in = jnp.dot(normed.T, grad_before, preferred_element_type=jnp.float32)
    grad_normed = jnp.dot(grad_before, w_in.T, preferred_element_type=jnp.float32)
    grad_gain = lax.optimization_barrier(jnp.sum(grad_normed * unit_values, axis=0))
    grad_unit = grad_normed * gain
    grad_depth = inverse * (grad_unit - lax.optimization_barrier(jnp.mean(grad_unit, axis=1, keepdims=True)) - unit_values * lax.optimization_barrier(jnp.mean(grad_unit * unit_values, axis=1, keepdims=True)))
    grad_depth = grad_depth.reshape(count, side, side, chans)
    grad_kernel = jnp.stack([lax.optimization_barrier(jnp.sum(grad_depth * shifted[offset].astype(jnp.float32), axis=(0, 1, 2))) for offset in range(9)])
    return (embed, (grad_kernel, grad_gain, grad_in, grad_out))

def run_blocks(padded, cot_rows, kernel, gain, w_in, w_out, size):
    count = padded.shape[0]
    group = math.gcd(count, size)
    chans = padded.shape[3]
    hidden = w_in.shape[1]
    stacked = padded.reshape((count // group, group) + padded.shape[1:])
    cot_stack = cot_rows.reshape(count // group, group, cot_rows.shape[1])
    initial = (jnp.zeros((9, chans), jnp.float32), jnp.zeros((chans,), jnp.float32), jnp.zeros((chans, hidden), jnp.float32), jnp.zeros((hidden, chans), jnp.float32))

    def advance(carry, item):
        embed, grads = block_section(item[0], item[1], kernel, gain, w_in, w_out)
        return (jax.tree.map(lambda left, right: left + right, carry, grads), embed)
    totals, embeds = lax.scan(advance, initial, (stacked, cot_stack))
    return (embeds.reshape(count, chans), totals)

def reference(features, tissue_count, neighbors, worker_perm, rotation, kernel, gain, w_in, w_out, cotangent):
    slots = jnp.arange(TILES_DEV, dtype=jnp.int32)
    embeds = []
    totals = None
    for group in range(GROUPS):
        counts = tissue_count[group]
        start = jnp.cumsum(counts, dtype=jnp.int32) - counts
        valid = slots[None, :] < counts[:, None]
        shifted_rank = jnp.mod(start[:, None] + slots[None, :] + rotation[group], WORKS)
        worker = worker_perm[group][jnp.mod(shifted_rank, N_TILE)]
        position = worker * WORK_DEV + shifted_rank // N_TILE
        target = jnp.where(valid, position, WORKS).reshape(-1).astype(jnp.int32)
        source = jnp.zeros((WORKS,), jnp.int32).at[target].set(jnp.arange(SLOTS, dtype=jnp.int32), mode='drop')
        owned = features[group]
        padded = assemble(owned, border_rows(owned), neighbors[group])[source]
        embed, grads = run_blocks(padded, cotangent[group], kernel, gain, w_in, w_out, 16)
        embeds.append(embed)
        if totals is None:
            totals = grads
        else:
            totals = jax.tree.map(lambda left, right: left + right, totals, grads)
    return (jnp.stack(embeds), totals[0], totals[1], totals[2], totals[3])
```

```python
import functools

import jax
import jax.numpy as jnp
from jax import lax
from jax.experimental import pallas as pl
from jax.experimental.pallas import tpu as pltpu
from jax.sharding import PartitionSpec as P

HIGHEST = lax.Precision.HIGHEST
PITCH = 32
FIRST = 8
TILES_STEP = 4
SMALL_ROWS = 8
VMEM_BYTES = 56 * 1024 * 1024


def bits_of(count):
    return [1 << bit for bit in range(count.bit_length() - 1)]


def swap(value, axis, bit):
    count = lax.axis_size(axis)
    return lax.ppermute(value, axis, [(i, i ^ bit) for i in range(count)])


def strip_kernel(tiles, strips, wide):
    count, side = tiles.shape[0], tiles.shape[1]
    for index in range(count):
        strips[index, 0] = tiles[index, 0]
        strips[index, 1] = tiles[index, side - 1]
        base = index * side * side
        for row in range(side):
            wide[base + row * side : base + (row + 1) * side, :] = tiles[index, row].astype(jnp.float32)
        strips[index, 2] = wide[pl.ds(base, side, stride=side), :].astype(jnp.bfloat16)
        strips[index, 3] = wide[pl.ds(base + side - 1, side, stride=side), :].astype(jnp.bfloat16)


def border_strips(tiles):
    slots, side, _, chans = tiles.shape
    step = 16
    return pl.pallas_call(
        strip_kernel,
        grid=(slots // step,),
        in_specs=[pl.BlockSpec((step, side, side, chans), lambda i: (i, 0, 0, 0))],
        out_specs=pl.BlockSpec((step, 4, side, chans), lambda i: (i, 0, 0, 0)),
        out_shape=jax.ShapeDtypeStruct((slots, 4, side, chans), jnp.bfloat16),
        scratch_shapes=[pltpu.VMEM((step * side * side, chans), jnp.float32)],
    )(tiles)


def block_kernel(
    peers,
    work,
    parts,
    meta,
    dealing,
    links,
    feats,
    own,
    before_halo,
    after_halo,
    cot_all,
    kern,
    gain,
    w_in,
    w_in_t,
    w_out,
    w_out_t,
    embed_out,
    grad_out,
    pad,
    unit,
    invs,
    normed,
    gb,
    asum,
    csum,
    ge,
    ga,
    tap_sum,
    gain_sum,
    gi_sum,
    go_sum,
    place,
):
    slots, side = feats.shape[0], feats.shape[1]
    chans, hidden = w_in.shape
    pixels = side * side
    cot_rows = cot_all.shape[0] // peers
    count, begin, me, mine = meta[0], meta[1], meta[2], meta[3]
    tap_sum[...] = jnp.zeros_like(tap_sum)
    gain_sum[...] = jnp.zeros_like(gain_sum)
    gi_sum[...] = jnp.zeros_like(gi_sum)
    asum[...] = jnp.zeros_like(asum)
    csum[...] = jnp.zeros_like(csum)
    ge[...] = jnp.zeros_like(ge)
    embed_out[...] = jnp.zeros_like(embed_out)

    @pl.loop(0, count)
    def _(slot):
        rank = lax.rem(begin + slot, peers * work)
        worker = dealing[lax.rem(rank, peers)]
        row = lax.div(rank, peers)
        block = worker ^ me
        place[slot] = block * work + row
        ge[pl.ds(slot, 1), :] = cot_all[pl.ds(block * cot_rows + row, 1), :] * (1.0 / pixels)

    ga[...] = 0.5 * jnp.dot(
        ge[...], w_out_t[...].astype(jnp.float32), precision=HIGHEST, preferred_element_type=jnp.float32
    )
    gains = gain[...]
    taps = [jnp.broadcast_to(kern[i : i + 1, :], (side, chans)) for i in range(9)]

    def strip(column, which, slot):
        index = links[column, slot] - (me - 1) * slots
        held = links[column, slot] >= 0
        first = before_halo[jnp.clip(index, 0, slots - 1), which]
        middle = own[jnp.clip(index - slots, 0, slots - 1), which]
        last = after_halo[jnp.clip(index - 2 * slots, 0, slots - 1), which]
        chosen = jnp.where(index < slots, first, jnp.where(index < 2 * slots, middle, last)).astype(jnp.float32)
        return jnp.where(held, chosen, 0.0)

    @pl.loop(0, lax.div(count + TILES_STEP - 1, TILES_STEP))
    def _(step):
        for part in range(TILES_STEP):
            slot = step * TILES_STEP + part
            base = part * (side + 2) * PITCH
            total = jnp.zeros((side, chans), jnp.float32)
            for y in range(side):
                row = feats[slot, y].astype(jnp.float32)
                pad[pl.ds(base + (y + 1) * PITCH + FIRST, side), :] = row
                total = total + row
            csum[pl.ds(slot, 1), :] = jnp.sum(total, axis=0, keepdims=True)
            top = base
            low = base + (side + 1) * PITCH
            left, right = FIRST - 1, FIRST + side
            pad[pl.ds(top + FIRST, side), :] = strip(0, 1, slot)
            pad[pl.ds(low + FIRST, side), :] = strip(1, 0, slot)
            pad[pl.ds(top + PITCH + left, side, stride=PITCH), :] = strip(2, 3, slot)
            pad[pl.ds(top + PITCH + right, side, stride=PITCH), :] = strip(3, 2, slot)
            pad[pl.ds(top + left, 1), :] = strip(4, 1, slot)[side - 1 :]
            pad[pl.ds(top + right, 1), :] = strip(5, 1, slot)[:1]
            pad[pl.ds(low + left, 1), :] = strip(6, 0, slot)[side - 1 :]
            pad[pl.ds(low + right, 1), :] = strip(7, 0, slot)[:1]
            for y in range(side):
                depth = None
                for a in range(3):
                    for b in range(3):
                        term = pad[pl.ds(base + (y + a) * PITCH + left + b, side), :] * taps[3 * a + b]
                        depth = term if depth is None else depth + term
                centered = depth - jnp.mean(depth, axis=1, keepdims=True)
                inverse = lax.rsqrt(jnp.mean(centered * centered, axis=1, keepdims=True) + 1e-06)
                units = centered * inverse
                at = part * pixels + y * side
                unit[at : at + side, :] = units
                invs[at : at + side, :] = jnp.broadcast_to(inverse, (side, chans))
                normed[at : at + side, :] = (units * gains).astype(jnp.bfloat16)
        for part in range(TILES_STEP):
            slot = step * TILES_STEP + part
            rows = slice(part * pixels, (part + 1) * pixels)
            before = jnp.dot(normed[rows, :], w_in[...], preferred_element_type=jnp.float32)
            scaled = before * 0.7071067811865476
            twice = 1.0 + lax.erf(scaled)
            bell = jnp.exp(-(scaled * scaled))
            asum[pl.ds(slot, 1), :] = 0.5 * jnp.sum(before * twice, axis=0, keepdims=True)
            slope = twice + (scaled * 1.1283791670955126) * bell
            gb[rows, :] = (slope * ga[pl.ds(slot, 1), :]).astype(jnp.bfloat16)
        gi_sum[...] += lax.dot_general(
            normed[...], gb[...], (((0,), (0,)), ((), ())), preferred_element_type=jnp.float32
        )
        gain_part = jnp.zeros((side, chans), jnp.float32)
        tap_part = [jnp.zeros((side, chans), jnp.float32) for _ in range(9)]
        for part in range(TILES_STEP):
            base = part * (side + 2) * PITCH
            grad_normed = jnp.dot(
                gb[part * pixels : (part + 1) * pixels, :], w_in_t[...], preferred_element_type=jnp.float32
            )
            for y in range(side):
                at = part * pixels + y * side
                rows = grad_normed[y * side : (y + 1) * side]
                units = unit[at : at + side, :]
                product = rows * units
                gain_part = gain_part + product
                grad_unit = rows * gains
                grad_depth = invs[at : at + side, :] * (
                    grad_unit
                    - jnp.mean(grad_unit, axis=1, keepdims=True)
                    - units * jnp.mean(product * gains, axis=1, keepdims=True)
                )
                for a in range(3):
                    for b in range(3):
                        tap_part[3 * a + b] = (
                            tap_part[3 * a + b]
                            + grad_depth * pad[pl.ds(base + (y + a) * PITCH + FIRST - 1 + b, side), :]
                        )
        gain_sum[...] += gain_part
        for i in range(9):
            tap_sum[i * side : (i + 1) * side, :] += tap_part[i]

    go_sum[...] = lax.dot_general(
        asum[...], ge[...], (((0,), (0,)), ((), ())), precision=HIGHEST, preferred_element_type=jnp.float32
    )
    projected = jnp.dot(
        asum[...], w_out[...].astype(jnp.float32), precision=HIGHEST, preferred_element_type=jnp.float32
    )
    csum[...] = (csum[...] + projected) * (1.0 / pixels)

    @pl.loop(0, count)
    def _(slot):
        embed_out[pl.ds(place[slot], 1), :] = csum[pl.ds(slot, 1), :]

    per = hidden // parts
    for block in range(parts):
        to = block ^ mine
        columns, offset = divmod(block * per, chans)
        grad_out[to, :per, :] = gi_sum[offset : offset + per, columns * chans : (columns + 1) * chans]
        grad_out[to, per : 2 * per, :] = go_sum[block * per : (block + 1) * per, :]
        grad_out[to, 2 * per :, :] = jnp.zeros((SMALL_ROWS, chans), jnp.float32)
    for i in range(9):
        grad_out[(i // SMALL_ROWS) ^ mine, pl.ds(2 * per + i % SMALL_ROWS, 1), :] = jnp.sum(
            tap_sum[i * side : (i + 1) * side, :], axis=0, keepdims=True
        )
    grad_out[1 ^ mine, pl.ds(2 * per + 1, 1), :] = jnp.sum(gain_sum[...], axis=0, keepdims=True)


def unpack_kernel(parts, meta, packed, gk, gg, gi, go):
    mine = meta[3]
    hidden, chans = go.shape
    per = hidden // parts
    for block in range(parts):
        at = block ^ mine
        columns, offset = divmod(block * per, chans)
        gi[offset : offset + per, columns * chans : (columns + 1) * chans] = packed[at, :per, :]
        go[block * per : (block + 1) * per, :] = packed[at, per : 2 * per, :]
    gk[:SMALL_ROWS, :] = packed[mine, 2 * per :, :]
    gk[SMALL_ROWS:9, :] = packed[1 ^ mine, 2 * per : 2 * per + 1, :]
    gg[...] = packed[1 ^ mine, 2 * per + 1 : 2 * per + 2, :]


def local(features, tissue_count, neighbors, worker_perm, rotation, kernel, gain, w_in, w_out, cotangent):
    feats = features[0]
    slots, side, _, chans = feats.shape
    hidden = w_in.shape[1]
    cot_rows = cotangent[0]
    work = cot_rows.shape[0]
    peers = lax.axis_size("tile")
    slides = lax.axis_size("slide")
    me = lax.axis_index("tile")
    slide_bits, tile_bits = bits_of(slides), bits_of(peers)
    halving = [("slide", bit) for bit in slide_bits] + [("tile", tile_bits[0])]
    parts = 1 << len(halving)
    mine = jnp.zeros((), jnp.int32)
    for place, (axis, bit) in enumerate(reversed(halving)):
        mine = mine + jnp.where((lax.axis_index(axis) & bit) > 0, 1 << place, 0)

    strips = border_strips(feats)
    before_halo = lax.ppermute(strips, "tile", [(i, i + 1) for i in range(peers - 1)])
    after_halo = lax.ppermute(strips, "tile", [(i + 1, i) for i in range(peers - 1)])

    gathered = jnp.concatenate(
        [cot_rows, jnp.broadcast_to(tissue_count.astype(jnp.float32), (8, chans))], axis=0
    )[None]
    for bit in tile_bits:
        gathered = jnp.concatenate([gathered, swap(gathered, "tile", bit)], axis=0)
    counts = gathered[:, work, 0].astype(jnp.int32)
    whose = jnp.arange(peers, dtype=jnp.int32) ^ me
    begin = jnp.sum(jnp.where(whose < me, counts, 0)) + rotation[0]
    meta = jnp.stack([tissue_count[0, 0], begin, me, mine]).astype(jnp.int32)

    f32 = jnp.float32
    pixels = side * side
    vmem = pl.BlockSpec(memory_space=pltpu.VMEM)
    smem = pl.BlockSpec(memory_space=pltpu.SMEM)
    per = hidden // parts
    block_rows = 2 * per + SMALL_ROWS
    embeds, packed = pl.pallas_call(
        functools.partial(block_kernel, peers, work, parts),
        in_specs=[smem] * 3 + [vmem] * 11,
        out_specs=[vmem] * 2,
        out_shape=[
            jax.ShapeDtypeStruct((peers * work, chans), f32),
            jax.ShapeDtypeStruct((parts, block_rows, chans), f32),
        ],
        scratch_shapes=[
            pltpu.VMEM((TILES_STEP * (side + 2) * PITCH, chans), f32),
            pltpu.VMEM((TILES_STEP * pixels, chans), f32),
            pltpu.VMEM((TILES_STEP * pixels, chans), f32),
            pltpu.VMEM((TILES_STEP * pixels, chans), jnp.bfloat16),
            pltpu.VMEM((TILES_STEP * pixels, hidden), jnp.bfloat16),
            pltpu.VMEM((slots, hidden), f32),
            pltpu.VMEM((slots, chans), f32),
            pltpu.VMEM((slots, chans), f32),
            pltpu.VMEM((slots, hidden), f32),
            pltpu.VMEM((9 * side, chans), f32),
            pltpu.VMEM((side, chans), f32),
            pltpu.VMEM((chans, hidden), f32),
            pltpu.VMEM((hidden, chans), f32),
            pltpu.SMEM((slots,), jnp.int32),
        ],
        compiler_params=pltpu.CompilerParams(vmem_limit_bytes=VMEM_BYTES),
    )(
        meta,
        worker_perm[0],
        neighbors[0].T,
        feats,
        strips,
        before_halo,
        after_halo,
        gathered.reshape(peers * (work + 8), chans),
        kernel.astype(f32),
        gain[None],
        w_in,
        w_in.T,
        w_out,
        w_out.T,
    )

    held = packed
    for axis, bit in halving[:-1]:
        half = held.shape[0] // 2
        held = held[:half] + swap(held[half:], axis, bit)
    embeds = embeds.reshape(peers, work, chans)
    for place, bit in enumerate(tile_bits):
        paired = embeds.reshape(embeds.shape[0] // 2, 2, work, chans)
        keep, send = paired[:, 0], paired[:, 1]
        if place == 0:
            mine_part, other_part = held[0], held[1]
        else:
            mine_part, other_part = held, held
        outgoing = jnp.concatenate([send.reshape(-1, chans), other_part], axis=0)
        incoming = swap(outgoing, "tile", bit)
        rows = send.shape[0] * work
        embeds = keep + incoming[:rows].reshape(keep.shape)
        held = mine_part + incoming[rows:]
    held = held[None]
    for axis, bit in reversed(halving):
        held = jnp.concatenate([held, swap(held, axis, bit)], axis=0)
    gk, gg, gi, go = pl.pallas_call(
        functools.partial(unpack_kernel, parts),
        in_specs=[smem, vmem],
        out_specs=[vmem] * 4,
        out_shape=[
            jax.ShapeDtypeStruct((9, chans), f32),
            jax.ShapeDtypeStruct((1, chans), f32),
            jax.ShapeDtypeStruct((chans, hidden), f32),
            jax.ShapeDtypeStruct((hidden, chans), f32),
        ],
    )(meta, held)
    return embeds, gk, gg[0], gi, go


def solution(mesh):
    placed = (
        P("slide", "tile", None, None, None),
        P("slide", "tile"),
        P("slide", "tile", None),
        P("slide", None),
        P("slide"),
        P(),
        P(),
        P(),
        P(),
        P("slide", "tile", None),
    )
    return jax.shard_map(
        local,
        mesh=mesh,
        in_specs=placed,
        out_specs=(P("slide", "tile", None), P(), P(), P(), P()),
        check_vma=False,
    )
```

```python
import functools

import jax
import jax.numpy as jnp
from jax import lax
from jax.experimental import pallas as pl
from jax.experimental.pallas import tpu as pltpu
from jax.sharding import PartitionSpec as P

HIGHEST = lax.Precision.HIGHEST
FIRST = 8
INNER_PITCH = 24
LINE_PITCH = 32
INNER_TILES = 4
BORDER_TILES = 8
SMALL_ROWS = 8
VMEM_BYTES = 24 * 1024 * 1024


def bits_of(count):
    return [1 << bit for bit in range(count.bit_length() - 1)]


def swap(value, axis, bit):
    count = lax.axis_size(axis)
    return lax.ppermute(value, axis, [(i, i ^ bit) for i in range(count)])


def strip_kernel(tiles, strips, inner, wide):
    count, side = tiles.shape[0], tiles.shape[1]
    for index in range(count):
        base = index * side * side
        for row in range(side):
            wide[base + row * side : base + (row + 1) * side, :] = tiles[index, row].astype(jnp.float32)
        for target, first, last in ((strips, 0, side - 1), (inner, 1, side - 2)):
            target[index, 0] = tiles[index, first]
            target[index, 1] = tiles[index, last]
            target[index, 2] = wide[pl.ds(base + first, side, stride=side), :].astype(jnp.bfloat16)
            target[index, 3] = wide[pl.ds(base + last, side, stride=side), :].astype(jnp.bfloat16)


def border_strips(tiles):
    slots, side, _, chans = tiles.shape
    step = 16
    shape = jax.ShapeDtypeStruct((slots, 4, side, chans), jnp.bfloat16)
    spec = pl.BlockSpec((step, 4, side, chans), lambda i: (i, 0, 0, 0))
    return pl.pallas_call(
        strip_kernel,
        grid=(slots // step,),
        in_specs=[pl.BlockSpec((step, side, side, chans), lambda i: (i, 0, 0, 0))],
        out_specs=[spec, spec],
        out_shape=[shape, shape],
        scratch_shapes=[pltpu.VMEM((step * side * side, chans), jnp.float32)],
    )(tiles)


def spread(rows, lines):
    return rows.reshape(lines, rows.shape[0] // lines, rows.shape[1])


def run_lines(
    step, tiles, starts, masked, weights, state, sums
):
    kern, gains, w_in, w_in_t = weights
    pad, unit, invs, normed, gb = state
    asum, ga, tap_sum, gain_sum, gi_sum = sums
    lines = len(starts)
    pad_rows = pad.shape[0] // tiles
    pixels = normed.shape[0] // tiles
    side = pixels // lines
    chans, hidden = w_in.shape
    taps = [jnp.broadcast_to(kern[i : i + 1, :], (side, chans)) for i in range(9)]
    place = lax.broadcasted_iota(jnp.int32, (side, hidden), 0)
    inside = jnp.where((place > 0) & (place < side - 1), 1.0, 0.0)
    for part in range(tiles):
        base = part * pad_rows
        for line in range(lines):
            depth = None
            for tap in range(9):
                term = pad[pl.ds(base + starts[line][tap], side), :] * taps[tap]
                depth = term if depth is None else depth + term
            centered = depth - jnp.mean(depth, axis=1, keepdims=True)
            inverse = lax.rsqrt(jnp.mean(centered * centered, axis=1, keepdims=True) + 1e-06)
            units = centered * inverse
            at = part * pixels + line * side
            unit[at : at + side, :] = units
            invs[at : at + side, :] = jnp.broadcast_to(inverse, (side, chans))
            normed[at : at + side, :] = (units * gains).astype(jnp.bfloat16)
    for part in range(tiles):
        slot = step * tiles + part
        rows = slice(part * pixels, (part + 1) * pixels)
        before = jnp.dot(normed[rows, :], w_in[...], preferred_element_type=jnp.float32)
        scaled = before * 0.7071067811865476
        twice = 1.0 + lax.erf(scaled)
        bell = jnp.exp(-(scaled * scaled))
        act = spread(before * twice, lines)
        slope = spread(twice + (scaled * 1.1283791670955126) * bell, lines)
        factor = jnp.broadcast_to(ga[pl.ds(slot, 1), :], (side, hidden))
        factor_inside = factor * inside
        whole = [act[line] for line in range(lines) if not masked[line]]
        partial = [act[line] for line in range(lines) if masked[line]]
        total = functools.reduce(jnp.add, partial) * inside
        if whole:
            total = total + functools.reduce(jnp.add, whole)
        asum[pl.ds(slot, 1), :] += jnp.sum(total, axis=0, keepdims=True)
        for line in range(lines):
            at = part * pixels + line * side
            gb[at : at + side, :] = (slope[line] * (factor_inside if masked[line] else factor)).astype(jnp.bfloat16)
    gi_sum[...] += lax.dot_general(normed[...], gb[...], (((0,), (0,)), ((), ())), preferred_element_type=jnp.float32)
    gain_part = jnp.zeros((side, chans), jnp.float32)
    tap_part = [jnp.zeros((side, chans), jnp.float32) for _ in range(9)]
    for part in range(tiles):
        base = part * pad_rows
        grad_normed = jnp.dot(
            gb[part * pixels : (part + 1) * pixels, :], w_in_t[...], preferred_element_type=jnp.float32
        )
        for line in range(lines):
            at = part * pixels + line * side
            rows = grad_normed[line * side : (line + 1) * side]
            units = unit[at : at + side, :]
            product = rows * units
            gain_part = gain_part + product
            grad_unit = rows * gains
            grad_depth = invs[at : at + side, :] * (
                grad_unit
                - jnp.mean(grad_unit, axis=1, keepdims=True)
                - units * jnp.mean(product * gains, axis=1, keepdims=True)
            )
            for tap in range(9):
                tap_part[tap] = tap_part[tap] + grad_depth * pad[pl.ds(base + starts[line][tap], side), :]
    gain_sum[...] += gain_part
    for tap in range(9):
        tap_sum[tap * side : (tap + 1) * side, :] += tap_part[tap]


def inner_kernel(
    peers,
    work,
    meta,
    dealing,
    feats,
    cot_all,
    kern,
    gain,
    w_in,
    w_in_t,
    w_out_t,
    asum,
    csum,
    ge,
    ga,
    tap_sum,
    gain_sum,
    gi_sum,
    pad,
    unit,
    invs,
    normed,
    gb,
):
    side = feats.shape[1]
    chans = feats.shape[3]
    pixels = side * side
    cot_rows = cot_all.shape[0] // peers
    count, begin, me = meta[0], meta[1], meta[2]
    for ref in (asum, csum, ge, tap_sum, gain_sum, gi_sum, pad):
        ref[...] = jnp.zeros_like(ref)

    @pl.loop(0, count)
    def _(slot):
        rank = lax.rem(begin + slot, peers * work)
        block = dealing[lax.rem(rank, peers)] ^ me
        row = block * cot_rows + lax.div(rank, peers)
        ge[pl.ds(slot, 1), :] = cot_all[pl.ds(row, 1), :] * (1.0 / pixels)

    ga[...] = 0.5 * jnp.dot(
        ge[...], w_out_t[...].astype(jnp.float32), precision=HIGHEST, preferred_element_type=jnp.float32
    )
    starts = [
        [(y - 1 + a) * INNER_PITCH + FIRST - 1 + b for a in range(3) for b in range(3)] for y in range(1, side - 1)
    ]

    @pl.loop(0, lax.div(count + INNER_TILES - 1, INNER_TILES))
    def _(step):
        for part in range(INNER_TILES):
            slot = step * INNER_TILES + part
            base = part * (pad.shape[0] // INNER_TILES)
            total = jnp.zeros((side, chans), jnp.float32)
            for y in range(side):
                row = feats[slot, y].astype(jnp.float32)
                pad[pl.ds(base + y * INNER_PITCH + FIRST, side), :] = row
                total = total + row
            csum[pl.ds(slot, 1), :] = jnp.sum(total, axis=0, keepdims=True)
        run_lines(
            step,
            INNER_TILES,
            starts,
            [True] * len(starts),
            (kern, gain[...], w_in, w_in_t),
            (pad, unit, invs, normed, gb),
            (asum, ga, tap_sum, gain_sum, gi_sum),
        )


def border_kernel(
    peers,
    work,
    parts,
    meta,
    dealing,
    links,
    own,
    inner,
    before_halo,
    after_halo,
    kern,
    gain,
    w_in,
    w_in_t,
    w_out,
    asum_in,
    csum,
    ge,
    ga,
    tap_in,
    gain_in,
    gi_in,
    embed_out,
    grad_out,
    pad,
    unit,
    invs,
    normed,
    gb,
    asum,
    tap_sum,
    gain_sum,
    gi_sum,
    go_sum,
    rows_out,
):
    slots, _, side, chans = own.shape
    hidden = w_in.shape[1]
    pixels = side * side
    count, begin, me, mine = meta[0], meta[1], meta[2], meta[3]
    for target, source in ((asum, asum_in), (tap_sum, tap_in), (gain_sum, gain_in), (gi_sum, gi_in)):
        target[...] = source[...]
    embed_out[...] = jnp.zeros_like(embed_out)

    def strip(column, which, slot):
        link = links[column, slot]
        index = link - (me - 1) * slots
        first = before_halo[jnp.clip(index, 0, slots - 1), which]
        middle = own[jnp.clip(index - slots, 0, slots - 1), which]
        last = after_halo[jnp.clip(index - 2 * slots, 0, slots - 1), which]
        chosen = jnp.where(index < slots, first, jnp.where(index < 2 * slots, middle, last)).astype(jnp.float32)
        return jnp.where(link >= 0, chosen, 0.0)

    across = [a * LINE_PITCH + FIRST - 1 + b for a in range(3) for b in range(3)]
    along = [b * LINE_PITCH + FIRST - 1 + a for a in range(3) for b in range(3)]
    starts = [
        [panel * 3 * LINE_PITCH + start for start in (across if panel < 2 else along)] for panel in range(4)
    ]

    @pl.loop(0, lax.div(count + BORDER_TILES - 1, BORDER_TILES))
    def _(step):
        for part in range(BORDER_TILES):
            slot = step * BORDER_TILES + part
            base = part * (pad.shape[0] // BORDER_TILES)
            up, down, left, right = strip(0, 1, slot), strip(1, 0, slot), strip(2, 3, slot), strip(3, 2, slot)
            upper_left, upper_right = strip(4, 1, slot)[side - 1 :], strip(5, 1, slot)[:1]
            lower_left, lower_right = strip(6, 0, slot)[side - 1 :], strip(7, 0, slot)[:1]
            rows = [own[slot, i].astype(jnp.float32) for i in range(4)]
            deep = [inner[slot, i].astype(jnp.float32) for i in range(4)]

            def cut(line, at):
                return line[at : at + 1]

            end = side - 1
            panels = (
                (
                    (upper_left, up, upper_right),
                    (cut(left, 0), rows[0], cut(right, 0)),
                    (cut(left, 1), deep[0], cut(right, 1)),
                ),
                (
                    (cut(left, end - 1), deep[1], cut(right, end - 1)),
                    (cut(left, end), rows[1], cut(right, end)),
                    (lower_left, down, lower_right),
                ),
                (
                    (upper_left, left, lower_left),
                    (cut(up, 0), rows[2], cut(down, 0)),
                    (cut(up, 1), deep[2], cut(down, 1)),
                ),
                (
                    (cut(up, end - 1), deep[3], cut(down, end - 1)),
                    (cut(up, end), rows[3], cut(down, end)),
                    (upper_right, right, lower_right),
                ),
            )
            for panel in range(4):
                for line in range(3):
                    at = base + (panel * 3 + line) * LINE_PITCH + FIRST
                    head, body, tail = panels[panel][line]
                    pad[pl.ds(at - 1, 1), :] = head
                    pad[pl.ds(at, side), :] = body
                    pad[pl.ds(at + side, 1), :] = tail
        run_lines(
            step,
            BORDER_TILES,
            starts,
            [False, False, True, True],
            (kern, gain[...], w_in, w_in_t),
            (pad, unit, invs, normed, gb),
            (asum, ga, tap_sum, gain_sum, gi_sum),
        )

    asum[...] = 0.5 * asum[...]
    go_sum[...] = lax.dot_general(
        asum[...], ge[...], (((0,), (0,)), ((), ())), precision=HIGHEST, preferred_element_type=jnp.float32
    )
    projected = jnp.dot(
        asum[...], w_out[...].astype(jnp.float32), precision=HIGHEST, preferred_element_type=jnp.float32
    )
    rows_out[...] = (csum[...] + projected) * (1.0 / pixels)

    @pl.loop(0, count)
    def _(slot):
        rank = lax.rem(begin + slot, peers * work)
        block = dealing[lax.rem(rank, peers)] ^ me
        embed_out[pl.ds(block * work + lax.div(rank, peers), 1), :] = rows_out[pl.ds(slot, 1), :]

    per = hidden // parts
    for block in range(parts):
        to = block ^ mine
        columns, offset = divmod(block * per, chans)
        grad_out[to, :per, :] = gi_sum[offset : offset + per, columns * chans : (columns + 1) * chans]
        grad_out[to, per : 2 * per, :] = go_sum[block * per : (block + 1) * per, :]
        grad_out[to, 2 * per :, :] = jnp.zeros((SMALL_ROWS, chans), jnp.float32)
    for i in range(9):
        grad_out[(i // SMALL_ROWS) ^ mine, pl.ds(2 * per + i % SMALL_ROWS, 1), :] = jnp.sum(
            tap_sum[i * side : (i + 1) * side, :], axis=0, keepdims=True
        )
    grad_out[1 ^ mine, pl.ds(2 * per + 1, 1), :] = jnp.sum(gain_sum[...], axis=0, keepdims=True)


def unpack_kernel(parts, meta, packed, gk, gg, gi, go):
    mine = meta[3]
    hidden, chans = go.shape
    per = hidden // parts
    for block in range(parts):
        at = block ^ mine
        columns, offset = divmod(block * per, chans)
        gi[offset : offset + per, columns * chans : (columns + 1) * chans] = packed[at, :per, :]
        go[block * per : (block + 1) * per, :] = packed[at, per : 2 * per, :]
    gk[:SMALL_ROWS, :] = packed[mine, 2 * per :, :]
    gk[SMALL_ROWS:9, :] = packed[1 ^ mine, 2 * per : 2 * per + 1, :]
    gg[...] = packed[1 ^ mine, 2 * per + 1 : 2 * per + 2, :]


def local(features, tissue_count, neighbors, worker_perm, rotation, kernel, gain, w_in, w_out, cotangent):
    feats = features[0]
    slots, side, _, chans = feats.shape
    hidden = w_in.shape[1]
    cot_rows = cotangent[0]
    work = cot_rows.shape[0]
    peers = lax.axis_size("tile")
    slides = lax.axis_size("slide")
    me = lax.axis_index("tile")
    slide_bits, tile_bits = bits_of(slides), bits_of(peers)
    halving = [("slide", bit) for bit in slide_bits] + [("tile", tile_bits[0])]
    parts = 1 << len(halving)
    mine = jnp.zeros((), jnp.int32)
    for place, (axis, bit) in enumerate(reversed(halving)):
        mine = mine + jnp.where((lax.axis_index(axis) & bit) > 0, 1 << place, 0)

    strips, inner = border_strips(feats)
    gathered = jnp.concatenate(
        [cot_rows, jnp.broadcast_to(tissue_count.astype(jnp.float32), (8, chans))], axis=0
    )[None]
    for bit in tile_bits:
        gathered = jnp.concatenate([gathered, swap(gathered, "tile", bit)], axis=0)
    gathered, strips = lax.optimization_barrier((gathered, strips))
    before_halo = lax.ppermute(strips, "tile", [(i, i + 1) for i in range(peers - 1)])
    after_halo = lax.ppermute(strips, "tile", [(i + 1, i) for i in range(peers - 1)])

    counts = gathered[:, work, 0].astype(jnp.int32)
    whose = jnp.arange(peers, dtype=jnp.int32) ^ me
    begin = jnp.sum(jnp.where(whose < me, counts, 0)) + rotation[0]
    meta = jnp.stack([tissue_count[0, 0], begin, me, mine]).astype(jnp.int32)

    f32 = jnp.float32
    vmem = pl.BlockSpec(memory_space=pltpu.VMEM)
    smem = pl.BlockSpec(memory_space=pltpu.SMEM)
    shape = jax.ShapeDtypeStruct
    params = pltpu.CompilerParams(vmem_limit_bytes=VMEM_BYTES)
    taps, gains, w_in_t = kernel.astype(f32), gain[None], w_in.T
    per = hidden // parts
    block_rows = 2 * per + SMALL_ROWS

    def line_scratch(pad_rows, pixels):
        return [
            pltpu.VMEM((pad_rows, chans), f32),
            pltpu.VMEM((pixels, chans), f32),
            pltpu.VMEM((pixels, chans), f32),
            pltpu.VMEM((pixels, chans), jnp.bfloat16),
            pltpu.VMEM((pixels, hidden), jnp.bfloat16),
        ]

    asum, csum, ge, ga, tap_sum, gain_sum, gi_sum = pl.pallas_call(
        functools.partial(inner_kernel, peers, work),
        in_specs=[smem] * 2 + [vmem] * 7,
        out_specs=[vmem] * 7,
        out_shape=[
            shape((slots, hidden), f32),
            shape((slots, chans), f32),
            shape((slots, chans), f32),
            shape((slots, hidden), f32),
            shape((9 * side, chans), f32),
            shape((side, chans), f32),
            shape((chans, hidden), f32),
        ],
        scratch_shapes=line_scratch(INNER_TILES * (side + 1) * INNER_PITCH, INNER_TILES * side * (side - 2)),
        compiler_params=params,
        cost_estimate=pl.CostEstimate(flops=30 * 10**9, bytes_accessed=10**7, transcendentals=10**7),
    )(
        meta,
        worker_perm[0],
        feats,
        gathered.reshape(peers * (work + 8), chans),
        taps,
        gains,
        w_in,
        w_in_t,
        w_out.T,
    )
    embeds, packed = pl.pallas_call(
        functools.partial(border_kernel, peers, work, parts),
        in_specs=[smem] * 3 + [vmem] * 16,
        out_specs=[vmem] * 2,
        out_shape=[shape((peers * work, chans), f32), shape((parts, block_rows, chans), f32)],
        scratch_shapes=line_scratch(BORDER_TILES * 12 * LINE_PITCH, BORDER_TILES * 4 * side)
        + [
            pltpu.VMEM((slots, hidden), f32),
            pltpu.VMEM((9 * side, chans), f32),
            pltpu.VMEM((side, chans), f32),
            pltpu.VMEM((chans, hidden), f32),
            pltpu.VMEM((hidden, chans), f32),
            pltpu.VMEM((slots, chans), f32),
        ],
        compiler_params=params,
    )(
        meta,
        worker_perm[0],
        neighbors[0].T,
        strips,
        inner,
        before_halo,
        after_halo,
        taps,
        gains,
        w_in,
        w_in_t,
        w_out,
        asum,
        csum,
        ge,
        ga,
        tap_sum,
        gain_sum,
        gi_sum,
    )

    held = packed
    for axis, bit in halving[:-1]:
        half = held.shape[0] // 2
        held = held[:half] + swap(held[half:], axis, bit)
    embeds = embeds.reshape(peers, work, chans)
    for place, bit in enumerate(tile_bits):
        paired = embeds.reshape(embeds.shape[0] // 2, 2, work, chans)
        keep, send = paired[:, 0], paired[:, 1]
        if place == 0:
            mine_part, other_part = held[0], held[1]
        else:
            mine_part, other_part = held, held
        outgoing = jnp.concatenate([send.reshape(-1, chans), other_part], axis=0)
        incoming = swap(outgoing, "tile", bit)
        rows = send.shape[0] * work
        embeds = keep + incoming[:rows].reshape(keep.shape)
        held = mine_part + incoming[rows:]
    held = held[None]
    for axis, bit in reversed(halving):
        held = jnp.concatenate([held, swap(held, axis, bit)], axis=0)
    gk, gg, gi, go = pl.pallas_call(
        functools.partial(unpack_kernel, parts),
        in_specs=[smem, vmem],
        out_specs=[vmem] * 4,
        out_shape=[
            jax.ShapeDtypeStruct((9, chans), f32),
            jax.ShapeDtypeStruct((1, chans), f32),
            jax.ShapeDtypeStruct((chans, hidden), f32),
            jax.ShapeDtypeStruct((hidden, chans), f32),
        ],
    )(meta, held)
    return embeds, gk, gg[0], gi, go


def solution(mesh):
    placed = (
        P("slide", "tile", None, None, None),
        P("slide", "tile"),
        P("slide", "tile", None),
        P("slide", None),
        P("slide"),
        P(),
        P(),
        P(),
        P(),
        P("slide", "tile", None),
    )
    return jax.shard_map(
        local,
        mesh=mesh,
        in_specs=placed,
        out_specs=(P("slide", "tile", None), P(), P(), P(), P()),
        check_vma=False,
    )
```

```python
import functools
import math

import jax
import jax.numpy as jnp
from jax import lax
from jax.experimental import pallas as pl
from jax.experimental.pallas import tpu as pltpu
from jax.sharding import PartitionSpec as P

HIGHEST = lax.Precision.HIGHEST
FIRST = 8
INNER_PITCH = 24
LINE_PITCH = 32
INNER_TILES = 4
BORDER_TILES = 8
SMALL_ROWS = 8
STRIP_TILES = 4
VMEM_BYTES = 24 * 1024 * 1024


def bits_of(count):
    return [1 << bit for bit in range(count.bit_length() - 1)]


def swap(value, axis, bit):
    count = lax.axis_size(axis)
    return lax.ppermute(value, axis, [(i, i ^ bit) for i in range(count)])


def strip_kernel(tiles, strips, inner, csum):
    slots, side, _, chans = tiles.shape
    columns = (0, side - 1, 1, side - 2)
    rows = (len(columns) + 1) * side
    row = lax.broadcasted_iota(jnp.int32, (rows, side * side), 0)
    pixel = lax.broadcasted_iota(jnp.int32, (rows, side * side), 1)
    group = lax.div(row, side)
    column = jnp.where(group == 0, columns[0], jnp.where(group == 1, columns[1], jnp.where(group == 2, columns[2], columns[3])))
    picked = (pixel == (row - group * side) * side + column) | (group == len(columns))
    select = jnp.where(picked, 1.0, 0.0).astype(jnp.bfloat16)

    @pl.loop(0, slots // STRIP_TILES)
    def _(step):
        for part in range(STRIP_TILES):
            slot = step * STRIP_TILES + part
            tile = tiles[slot].reshape(side * side, chans)
            found = jnp.dot(select, tile, preferred_element_type=jnp.float32)
            lines = found[: len(columns) * side].astype(jnp.bfloat16)
            strips[slot, 0] = tiles[slot, 0]
            strips[slot, 1] = tiles[slot, side - 1]
            strips[slot, 2] = lines[:side]
            strips[slot, 3] = lines[side : 2 * side]
            inner[slot, 0] = tiles[slot, 1]
            inner[slot, 1] = tiles[slot, side - 2]
            inner[slot, 2] = lines[2 * side : 3 * side]
            inner[slot, 3] = lines[3 * side :]
            csum[pl.ds(slot, 1), :] = found[len(columns) * side : len(columns) * side + 1]


def border_strips(tiles):
    slots, side, _, chans = tiles.shape
    shape = jax.ShapeDtypeStruct((slots, 4, side, chans), jnp.bfloat16)
    spec = pl.BlockSpec(memory_space=pltpu.VMEM)
    return pl.pallas_call(
        strip_kernel,
        in_specs=[spec],
        out_specs=[spec] * 3,
        out_shape=[shape, shape, jax.ShapeDtypeStruct((slots, chans), jnp.float32)],
        compiler_params=pltpu.CompilerParams(vmem_limit_bytes=VMEM_BYTES),
        cost_estimate=pl.CostEstimate(flops=10**9, bytes_accessed=10**7, transcendentals=0),
    )(tiles)


def spread(rows, lines):
    return rows.reshape(lines, rows.shape[0] // lines, rows.shape[1])


def run_lines(
    step, tiles, starts, masked, weights, state, sums
):
    kern, gains, w_in, w_in_t = weights
    pad, unit, invs, normed, gb = state
    asum, ga, tap_sum, gain_sum, gi_sum = sums
    lines = len(starts)
    pad_rows = pad.shape[0] // tiles
    pixels = normed.shape[0] // tiles
    side = pixels // lines
    chans, hidden = w_in.shape
    gains_root = gains * math.sqrt(chans)
    wide_taps = kern[...].astype(jnp.float32)
    taps = [jnp.broadcast_to(wide_taps[i : i + 1, :], (side, chans)) for i in range(9)]
    place = lax.broadcasted_iota(jnp.int32, (side, hidden), 0)
    inside = jnp.where((place > 0) & (place < side - 1), 1.0, 0.0)
    for part in range(tiles):
        base = part * pad_rows
        for line in range(lines):
            depth = None
            for tap in range(9):
                term = pad[pl.ds(base + starts[line][tap], side), :] * taps[tap]
                depth = term if depth is None else depth + term
            centered = depth - jnp.mean(depth, axis=1, keepdims=True)
            inverse = lax.rsqrt(jnp.sum(centered * centered, axis=1, keepdims=True) + chans * 1e-06)
            units = centered * inverse
            at = part * pixels + line * side
            unit[at : at + side, :] = units
            invs[at : at + side, :] = jnp.broadcast_to(inverse, (side, chans))
            normed[at : at + side, :] = (units * gains_root).astype(jnp.bfloat16)
    for part in range(tiles):
        slot = step * tiles + part
        rows = slice(part * pixels, (part + 1) * pixels)
        before = jnp.dot(normed[rows, :], w_in[...], preferred_element_type=jnp.float32)
        scaled = before * 0.7071067811865476
        twice = 1.0 + lax.erf(scaled)
        bell = jnp.exp2(scaled * scaled * -1.4426950408889634)
        act = spread(before * twice, lines)
        slope = spread(twice + (scaled * 1.1283791670955126) * bell, lines)
        factor = jnp.broadcast_to(ga[pl.ds(slot, 1), :], (side, hidden))
        factor_inside = factor * inside
        whole = [act[line] for line in range(lines) if not masked[line]]
        partial = [act[line] for line in range(lines) if masked[line]]
        total = functools.reduce(jnp.add, partial) * inside
        if whole:
            total = total + functools.reduce(jnp.add, whole)
        asum[pl.ds(slot, 1), :] += jnp.sum(total, axis=0, keepdims=True)
        for line in range(lines):
            at = part * pixels + line * side
            gb[at : at + side, :] = (slope[line] * (factor_inside if masked[line] else factor)).astype(jnp.bfloat16)
    gi_sum[...] += lax.dot_general(normed[...], gb[...], (((0,), (0,)), ((), ())), preferred_element_type=jnp.float32)
    gain_part = jnp.zeros((side, chans), jnp.float32)
    tap_part = [jnp.zeros((side, chans), jnp.float32) for _ in range(9)]
    for part in range(tiles):
        base = part * pad_rows
        grad_normed = jnp.dot(
            gb[part * pixels : (part + 1) * pixels, :], w_in_t[...], preferred_element_type=jnp.float32
        )
        for line in range(lines):
            at = part * pixels + line * side
            rows = grad_normed[line * side : (line + 1) * side]
            units = unit[at : at + side, :]
            product = rows * units
            gain_part = gain_part + product
            grad_unit = rows * gains
            grad_depth = invs[at : at + side, :] * (
                grad_unit
                - jnp.mean(grad_unit, axis=1, keepdims=True)
                - units * jnp.sum(product * gains, axis=1, keepdims=True)
            )
            for tap in range(9):
                tap_part[tap] = tap_part[tap] + grad_depth * pad[pl.ds(base + starts[line][tap], side), :]
    gain_sum[...] += gain_part
    for tap in range(9):
        tap_sum[tap * side : (tap + 1) * side, :] += tap_part[tap]


def inner_kernel(
    peers,
    work,
    meta,
    dealing,
    feats,
    cot_all,
    kern,
    gain,
    w_in,
    w_out,
    asum,
    ge,
    ga,
    tap_sum,
    gain_sum,
    gi_sum,
    w_in_t,
    pad,
    unit,
    invs,
    normed,
    gb,
):
    side = feats.shape[1]
    chans = feats.shape[3]
    pixels = side * side
    cot_rows = cot_all.shape[0] // peers
    count, begin, me = meta[0], meta[1], meta[2]
    for ref in (asum, ge, tap_sum, gain_sum, gi_sum, pad):
        ref[...] = jnp.zeros_like(ref)

    @pl.loop(0, count)
    def _(slot):
        rank = lax.rem(begin + slot, peers * work)
        block = dealing[lax.rem(rank, peers)] ^ me
        row = block * cot_rows + lax.div(rank, peers)
        ge[pl.ds(slot, 1), :] = cot_all[pl.ds(row, 1), :] * (1.0 / pixels)

    w_in_t[...] = w_in[...].astype(jnp.float32).T.astype(jnp.bfloat16)
    ga[...] = 0.5 * lax.dot_general(
        ge[...],
        w_out[...].astype(jnp.float32),
        (((1,), (1,)), ((), ())),
        precision=HIGHEST,
        preferred_element_type=jnp.float32,
    )
    starts = [
        [(y - 1 + a) * INNER_PITCH + FIRST - 1 + b for a in range(3) for b in range(3)] for y in range(1, side - 1)
    ]

    @pl.loop(0, lax.div(count + INNER_TILES - 1, INNER_TILES))
    def _(step):
        for part in range(INNER_TILES):
            slot = step * INNER_TILES + part
            base = part * (pad.shape[0] // INNER_TILES)
            for y in range(side):
                pad[pl.ds(base + y * INNER_PITCH + FIRST, side), :] = feats[slot, y].astype(jnp.float32)
        run_lines(
            step,
            INNER_TILES,
            starts,
            [True] * len(starts),
            (kern, gain[...], w_in, w_in_t),
            (pad, unit, invs, normed, gb),
            (asum, ga, tap_sum, gain_sum, gi_sum),
        )


def border_kernel(
    peers,
    work,
    parts,
    meta,
    dealing,
    links,
    own,
    inner,
    halo_pair,
    halo_cross,
    kern,
    gain,
    w_in,
    w_in_t,
    w_out,
    asum_in,
    csum,
    ge,
    ga,
    tap_in,
    gain_in,
    gi_in,
    embed_out,
    grad_out,
    pad,
    unit,
    invs,
    normed,
    gb,
    asum,
    tap_sum,
    gain_sum,
    gi_sum,
    go_sum,
    rows_out,
):
    slots, _, side, chans = own.shape
    hidden = w_in.shape[1]
    pixels = side * side
    count, begin, me, mine = meta[0], meta[1], meta[2], meta[3]
    for target, source in ((asum, asum_in), (tap_sum, tap_in), (gain_sum, gain_in), (gi_sum, gi_in)):
        target[...] = source[...]
    embed_out[...] = jnp.zeros_like(embed_out)

    paired = lax.rem(me, 2) * -2 + 1

    def strip(column, which, slot):
        link = links[column, slot]
        index = lax.rem(jnp.maximum(link, 0), slots)
        aside = lax.div(link, slots) - me
        here, pair, cross = own[index, which], halo_pair[index, which], halo_cross[index, which]
        chosen = jnp.where(aside == 0, here, jnp.where(aside == paired, pair, cross)).astype(jnp.float32)
        return jnp.where(link >= 0, chosen, 0.0)

    lines = side + 2
    plane = lines * LINE_PITCH
    across = [a * LINE_PITCH + FIRST - 1 + b for a in range(3) for b in range(3)]
    along = [plane + b * LINE_PITCH + FIRST - 1 + a for a in range(3) for b in range(3)]
    far = (side - 1) * LINE_PITCH
    starts = [
        across,
        [start + far for start in across],
        along,
        [start + far for start in along],
    ]

    @pl.loop(0, lax.div(count + BORDER_TILES - 1, BORDER_TILES))
    def _(step):
        for part in range(BORDER_TILES):
            slot = step * BORDER_TILES + part
            rows = part * (pad.shape[0] // BORDER_TILES) + FIRST
            columns = rows + plane
            up, down, left, right = strip(0, 1, slot), strip(1, 0, slot), strip(2, 3, slot), strip(3, 2, slot)
            edge = [own[slot, i].astype(jnp.float32) for i in range(4)]
            deep = [inner[slot, i].astype(jnp.float32) for i in range(4)]
            for at, bodies, head, tail in (
                (rows, (up, edge[0], deep[0], deep[1], edge[1], down), left, right),
                (columns, (left, edge[2], deep[2], deep[3], edge[3], right), up, down),
            ):
                for line, body in zip((0, 1, 2, side - 1, side, side + 1), bodies, strict=True):
                    pad[pl.ds(at + line * LINE_PITCH, side), :] = body
                pad[pl.ds(at + LINE_PITCH - 1, side, stride=LINE_PITCH), :] = head
                pad[pl.ds(at + LINE_PITCH + side, side, stride=LINE_PITCH), :] = tail
            last = (side + 1) * LINE_PITCH
            for corner, in_rows, in_columns in (
                (strip(4, 1, slot)[side - 1 :], -1, -1),
                (strip(5, 1, slot)[:1], side, last - 1),
                (strip(6, 0, slot)[side - 1 :], last - 1, side),
                (strip(7, 0, slot)[:1], last + side, last + side),
            ):
                pad[pl.ds(rows + in_rows, 1), :] = corner
                pad[pl.ds(columns + in_columns, 1), :] = corner
        run_lines(
            step,
            BORDER_TILES,
            starts,
            [False, False, True, True],
            (kern, gain[...], w_in, w_in_t),
            (pad, unit, invs, normed, gb),
            (asum, ga, tap_sum, gain_sum, gi_sum),
        )

    asum[...] = 0.5 * asum[...]
    go_sum[...] = lax.dot_general(
        asum[...], ge[...], (((0,), (0,)), ((), ())), precision=HIGHEST, preferred_element_type=jnp.float32
    )
    projected = jnp.dot(
        asum[...], w_out[...].astype(jnp.float32), precision=HIGHEST, preferred_element_type=jnp.float32
    )
    rows_out[...] = (csum[...] + projected) * (1.0 / pixels)

    @pl.loop(0, count)
    def _(slot):
        rank = lax.rem(begin + slot, peers * work)
        block = dealing[lax.rem(rank, peers)] ^ me
        embed_out[pl.ds(block * work + lax.div(rank, peers), 1), :] = rows_out[pl.ds(slot, 1), :]

    per = hidden // parts
    for block in range(parts):
        to = block ^ mine
        columns, offset = divmod(block * per, chans)
        grad_out[to, :per, :] = gi_sum[offset : offset + per, columns * chans : (columns + 1) * chans]
        grad_out[to, per : 2 * per, :] = go_sum[block * per : (block + 1) * per, :]
        grad_out[to, 2 * per :, :] = jnp.zeros((SMALL_ROWS, chans), jnp.float32)
    for i in range(9):
        grad_out[(i // SMALL_ROWS) ^ mine, pl.ds(2 * per + i % SMALL_ROWS, 1), :] = math.sqrt(chans) * jnp.sum(
            tap_sum[i * side : (i + 1) * side, :], axis=0, keepdims=True
        )
    grad_out[1 ^ mine, pl.ds(2 * per + 1, 1), :] = math.sqrt(chans) * jnp.sum(
        gain_sum[...], axis=0, keepdims=True
    )


def unpack_kernel(parts, meta, near, far, gk, gg, gi, go, packed):
    mine = meta[3]
    packed[: parts // 2] = near[...]
    packed[parts // 2 :] = far[...]
    hidden, chans = go.shape
    per = hidden // parts
    for block in range(parts):
        at = block ^ mine
        columns, offset = divmod(block * per, chans)
        gi[offset : offset + per, columns * chans : (columns + 1) * chans] = packed[at, :per, :]
        go[block * per : (block + 1) * per, :] = packed[at, per : 2 * per, :]
    gk[:SMALL_ROWS, :] = packed[mine, 2 * per :, :]
    gk[SMALL_ROWS:9, :] = packed[1 ^ mine, 2 * per : 2 * per + 1, :]
    gg[...] = packed[1 ^ mine, 2 * per + 1 : 2 * per + 2, :]


def local(features, tissue_count, neighbors, worker_perm, rotation, kernel, gain, w_in, w_out, cotangent):
    feats = features[0]
    slots, side, _, chans = feats.shape
    hidden = w_in.shape[1]
    cot_rows = cotangent[0]
    work = cot_rows.shape[0]
    peers = lax.axis_size("tile")
    slides = lax.axis_size("slide")
    me = lax.axis_index("tile")
    slide_bits, tile_bits = bits_of(slides), bits_of(peers)
    halving = [("slide", bit) for bit in slide_bits] + [("tile", tile_bits[0])]
    parts = 1 << len(halving)
    mine = jnp.zeros((), jnp.int32)
    for place, (axis, bit) in enumerate(reversed(halving)):
        mine = mine + jnp.where((lax.axis_index(axis) & bit) > 0, 1 << place, 0)

    strips, inner, csum = border_strips(feats)
    gathered = jnp.concatenate(
        [cot_rows, jnp.broadcast_to(tissue_count.astype(jnp.float32), (8, chans))], axis=0
    )[None]
    for bit in tile_bits:
        gathered = jnp.concatenate([gathered, swap(gathered, "tile", bit)], axis=0)
        if bit == 1:
            gathered, strips = lax.optimization_barrier((gathered, strips))
            halo_pair = swap(strips, "tile", 1)
    gathered, strips = lax.optimization_barrier((gathered, strips))
    cross = [(i, i + 1) for i in range(1, peers - 1, 2)]
    halo_cross = lax.ppermute(strips, "tile", cross + [(j, i) for i, j in cross])

    counts = gathered[:, work, 0].astype(jnp.int32)
    whose = jnp.arange(peers, dtype=jnp.int32) ^ me
    begin = jnp.sum(jnp.where(whose < me, counts, 0)) + rotation[0]
    meta = jnp.stack([tissue_count[0, 0], begin, me, mine]).astype(jnp.int32)

    f32 = jnp.float32
    vmem = pl.BlockSpec(memory_space=pltpu.VMEM)
    smem = pl.BlockSpec(memory_space=pltpu.SMEM)
    shape = jax.ShapeDtypeStruct
    params = pltpu.CompilerParams(vmem_limit_bytes=VMEM_BYTES)
    gains = gain[None]
    per = hidden // parts
    block_rows = 2 * per + SMALL_ROWS

    def line_scratch(pad_rows, pixels):
        return [
            pltpu.VMEM((pad_rows, chans), f32),
            pltpu.VMEM((pixels, chans), f32),
            pltpu.VMEM((pixels, chans), f32),
            pltpu.VMEM((pixels, chans), jnp.bfloat16),
            pltpu.VMEM((pixels, hidden), jnp.bfloat16),
        ]

    asum, ge, ga, tap_sum, gain_sum, gi_sum, w_in_t = pl.pallas_call(
        functools.partial(inner_kernel, peers, work),
        in_specs=[smem] * 2 + [vmem] * 6,
        out_specs=[vmem] * 7,
        out_shape=[
            shape((slots, hidden), f32),
            shape((slots, chans), f32),
            shape((slots, hidden), f32),
            shape((9 * side, chans), f32),
            shape((side, chans), f32),
            shape((chans, hidden), f32),
            shape((hidden, chans), jnp.bfloat16),
        ],
        scratch_shapes=line_scratch(INNER_TILES * (side + 1) * INNER_PITCH, INNER_TILES * side * (side - 2)),
        compiler_params=params,
    )(
        meta,
        worker_perm[0],
        feats,
        gathered.reshape(peers * (work + 8), chans),
        kernel,
        gains,
        w_in,
        w_out,
    )
    embeds, packed = pl.pallas_call(
        functools.partial(border_kernel, peers, work, parts),
        in_specs=[smem] * 3 + [vmem] * 16,
        out_specs=[vmem] * 2,
        out_shape=[shape((peers * work, chans), f32), shape((parts, block_rows, chans), f32)],
        scratch_shapes=line_scratch(BORDER_TILES * 2 * (side + 2) * LINE_PITCH, BORDER_TILES * 4 * side)
        + [
            pltpu.VMEM((slots, hidden), f32),
            pltpu.VMEM((9 * side, chans), f32),
            pltpu.VMEM((side, chans), f32),
            pltpu.VMEM((chans, hidden), f32),
            pltpu.VMEM((hidden, chans), f32),
            pltpu.VMEM((slots, chans), f32),
        ],
        compiler_params=params,
    )(
        meta,
        worker_perm[0],
        neighbors[0].T,
        strips,
        inner,
        halo_pair,
        halo_cross,
        kernel,
        gains,
        w_in,
        w_in_t,
        w_out,
        asum,
        csum,
        ge,
        ga,
        tap_sum,
        gain_sum,
        gi_sum,
    )

    held = packed
    for axis, bit in halving[:-1]:
        half = held.shape[0] // 2
        held = held[:half] + swap(held[half:], axis, bit)
    embeds = embeds.reshape(peers, work, chans)
    for place, bit in enumerate(tile_bits):
        paired = embeds.reshape(embeds.shape[0] // 2, 2, work, chans)
        keep, send = paired[:, 0], paired[:, 1]
        if place == 0:
            mine_part, other_part = held[0], held[1]
        else:
            mine_part, other_part = held, held
        outgoing = jnp.concatenate([send.reshape(-1, chans), other_part], axis=0)
        incoming = swap(outgoing, "tile", bit)
        rows = send.shape[0] * work
        embeds = keep + incoming[:rows].reshape(keep.shape)
        held = mine_part + incoming[rows:]
    held = held[None]
    for axis, bit in reversed(halving[1:]):
        held = jnp.concatenate([held, swap(held, axis, bit)], axis=0)
    far = swap(held, *halving[0])
    gk, gg, gi, go = pl.pallas_call(
        functools.partial(unpack_kernel, parts),
        in_specs=[smem, vmem, vmem],
        out_specs=[vmem] * 4,
        out_shape=[
            jax.ShapeDtypeStruct((9, chans), f32),
            jax.ShapeDtypeStruct((1, chans), f32),
            jax.ShapeDtypeStruct((chans, hidden), f32),
            jax.ShapeDtypeStruct((hidden, chans), f32),
        ],
        scratch_shapes=[pltpu.VMEM((parts, block_rows, chans), f32)],
        compiler_params=params,
    )(meta, held, far)
    return embeds, gk, gg[0], gi, go


def solution(mesh):
    placed = (
        P("slide", "tile", None, None, None),
        P("slide", "tile"),
        P("slide", "tile", None),
        P("slide", None),
        P("slide"),
        P(),
        P(),
        P(),
        P(),
        P("slide", "tile", None),
    )
    return jax.shard_map(
        local,
        mesh=mesh,
        in_specs=placed,
        out_specs=(P("slide", "tile", None), P(), P(), P(), P()),
        check_vma=False,
    )
```

```python
import functools
import math

import jax
import jax.numpy as jnp
from jax import lax
from jax.experimental import pallas as pl
from jax.experimental.pallas import tpu as pltpu
from jax.sharding import PartitionSpec as P

HIGHEST = lax.Precision.HIGHEST
FIRST = 8
INNER_PITCH = 24
LINE_PITCH = 32
INNER_TILES = 4
BORDER_TILES = 16
SMALL_ROWS = 8
STRIP_TILES = 4
VMEM_BYTES = 32 * 1024 * 1024


def bits_of(count):
    return [1 << bit for bit in range(count.bit_length() - 1)]


def swap(value, axis, bit):
    count = lax.axis_size(axis)
    return lax.ppermute(value, axis, [(i, i ^ bit) for i in range(count)])


def strip_kernel(tiles, held, strips, inner, csum):
    slots, side, _, chans = tiles.shape
    columns = (0, side - 1, 1, side - 2)
    rows = (len(columns) + 1) * side
    row = lax.broadcasted_iota(jnp.int32, (rows, side * side), 0)
    pixel = lax.broadcasted_iota(jnp.int32, (rows, side * side), 1)
    group = lax.div(row, side)
    column = jnp.where(group == 0, columns[0], jnp.where(group == 1, columns[1], jnp.where(group == 2, columns[2], columns[3])))
    picked = (pixel == (row - group * side) * side + column) | (group == len(columns))
    select = jnp.where(picked, 1.0, 0.0).astype(jnp.bfloat16)

    @pl.loop(0, slots // STRIP_TILES)
    def _(step):
        for part in range(STRIP_TILES):
            slot = step * STRIP_TILES + part
            tile = tiles[slot].reshape(side * side, chans)
            found = jnp.dot(select, tile, preferred_element_type=jnp.float32)
            lines = found[: len(columns) * side].astype(jnp.bfloat16)
            strips[slot, 0] = tiles[slot, 0]
            strips[slot, 1] = tiles[slot, side - 1]
            strips[slot, 2] = lines[:side]
            strips[slot, 3] = lines[side : 2 * side]
            inner[slot, 0] = tiles[slot, 1]
            inner[slot, 1] = tiles[slot, side - 2]
            inner[slot, 2] = lines[2 * side : 3 * side]
            inner[slot, 3] = lines[3 * side :]
            csum[pl.ds(slot, 1), :] = found[len(columns) * side : len(columns) * side + 1]


def border_strips(tiles):
    slots, side, _, chans = tiles.shape
    shape = jax.ShapeDtypeStruct((slots, 4, side, chans), jnp.bfloat16)
    spec = pl.BlockSpec(memory_space=pltpu.VMEM)
    return pl.pallas_call(
        strip_kernel,
        in_specs=[spec],
        out_specs=[spec] * 4,
        out_shape=[
            jax.ShapeDtypeStruct(tiles.shape, tiles.dtype),
            shape,
            shape,
            jax.ShapeDtypeStruct((slots, chans), jnp.float32),
        ],
        input_output_aliases={0: 0},
        compiler_params=pltpu.CompilerParams(vmem_limit_bytes=VMEM_BYTES),
        cost_estimate=pl.CostEstimate(flops=10**9, bytes_accessed=10**7, transcendentals=0),
    )(tiles)


def spread(rows, lines):
    return rows.reshape(lines, rows.shape[0] // lines, rows.shape[1])


def run_lines(
    step, tiles, starts, masked, weights, state, sums
):
    kern, gains, w_gelu, w_in_t = weights
    pad, unit, invs, normed, gb, back = state
    asum, ga, tap_sum, gain_sum, gi_sum = sums
    lines = len(starts)
    pad_rows = pad.shape[0] // tiles
    pixels = normed.shape[0] // tiles
    side = pixels // lines
    hidden, chans = w_in_t.shape
    half = side // 2
    gains_root = gains * math.sqrt(chans)
    wide_taps = kern[...].astype(jnp.float32)
    taps = [jnp.broadcast_to(wide_taps[i : i + 1, :], (side, chans)) for i in range(9)]
    place = lax.broadcasted_iota(jnp.int32, (side, hidden), 0)
    inside = jnp.where((place > 0) & (place < side - 1), 1.0, 0.0)
    for part in range(tiles):
        base = part * pad_rows
        for line in range(lines):
            depth = None
            for tap in range(9):
                term = pad[pl.ds(base + starts[line][tap], side), :] * taps[tap]
                depth = term if depth is None else depth + term
            centered = depth - jnp.mean(depth, axis=1, keepdims=True)
            inverse = lax.rsqrt(jnp.sum(centered * centered, axis=1, keepdims=True) + chans * 1e-06)
            units = centered * inverse
            at = part * pixels + line * side
            unit[at : at + side, :] = units
            invs[at : at + side, :] = jnp.broadcast_to(inverse, (side, chans))
            normed[at : at + side, :] = (units * gains_root).astype(jnp.bfloat16)
    for part in range(tiles):
        slot = step * tiles + part
        rows = slice(part * pixels, (part + 1) * pixels)
        doubled = jnp.concatenate([normed[rows, :]] * 2, axis=1)
        scaled = jnp.dot(doubled, w_gelu[...], preferred_element_type=jnp.float32)
        twice = 1.0 + lax.erf(scaled)
        bell = jnp.exp2(scaled * scaled * -1.4426950408889634)
        act = spread(scaled * twice, lines)
        slope = spread(twice + (scaled * 1.1283791670955126) * bell, lines)
        factor = jnp.broadcast_to(ga[pl.ds(slot, 1), :], (side, hidden))
        factor_inside = factor * inside
        whole = [act[line] for line in range(lines) if not masked[line]]
        partial = [act[line] for line in range(lines) if masked[line]]
        total = functools.reduce(jnp.add, partial) * inside
        if whole:
            total = total + functools.reduce(jnp.add, whole)
        asum[pl.ds(slot, 1), :] += jnp.sum(total, axis=0, keepdims=True)
        for line in range(lines):
            at = part * pixels + line * side
            gb[at : at + side, :] = (slope[line] * (factor_inside if masked[line] else factor)).astype(jnp.bfloat16)
    back[...] = jnp.dot(gb[...], w_in_t[...], preferred_element_type=jnp.float32)
    gi_sum[...] += lax.dot_general(normed[...], gb[...], (((0,), (0,)), ((), ())), preferred_element_type=jnp.float32)
    gain_part = jnp.zeros((half, chans), jnp.float32)
    tap_part = [jnp.zeros((half, chans), jnp.float32) for _ in range(9)]
    for part in range(tiles):
        base = part * pad_rows
        for line in range(lines):
            at = part * pixels + line * side
            units = unit[at : at + side, :]
            grad_unit = back[at : at + side, :] * gains
            product = grad_unit * units
            gain_part = gain_part + (product[:half] + product[half:])
            grad_depth = invs[at : at + side, :] * (
                grad_unit
                - jnp.mean(grad_unit, axis=1, keepdims=True)
                - units * jnp.sum(product, axis=1, keepdims=True)
            )
            for tap in range(9):
                term = grad_depth * pad[pl.ds(base + starts[line][tap], side), :]
                tap_part[tap] = tap_part[tap] + (term[:half] + term[half:])
    gain_sum[...] += gain_part
    for tap in range(9):
        tap_sum[tap * half : (tap + 1) * half, :] += tap_part[tap]


def line_scratch(tiles, pad_rows, lines, side, chans, hidden):
    f32, bf16 = jnp.float32, jnp.bfloat16
    pixels = tiles * lines * side
    return [
        pltpu.VMEM((tiles * pad_rows, chans), f32),
        pltpu.VMEM((pixels, chans), f32),
        pltpu.VMEM((pixels, chans), f32),
        pltpu.VMEM((pixels, chans), bf16),
        pltpu.VMEM((pixels, hidden), bf16),
        pltpu.VMEM((pixels, chans), f32),
        pltpu.VMEM((2 * chans, hidden), bf16),
    ]


def split_weights(w_in, w_gelu):
    chans = w_in.shape[0]
    scaled = w_in[...].astype(jnp.float32) * 0.7071067811865476
    high = scaled.astype(jnp.bfloat16)
    w_gelu[:chans, :] = high
    w_gelu[chans:, :] = (scaled - high.astype(jnp.float32)).astype(jnp.bfloat16)


def inner_kernel(
    peers,
    work,
    meta,
    dealing,
    feats,
    cot_all,
    kern,
    gain,
    w_in,
    w_out,
    asum,
    ge,
    ga,
    tap_sum,
    gain_sum,
    gi_sum,
    w_in_t,
    pad,
    unit,
    invs,
    normed,
    gb,
    back,
    w_gelu,
):
    side = feats.shape[1]
    chans = feats.shape[3]
    pixels = side * side
    cot_rows = cot_all.shape[0] // peers
    count, begin, me = meta[0], meta[1], meta[2]
    split_weights(w_in, w_gelu)
    for ref in (asum, ge, tap_sum, gain_sum, gi_sum, pad):
        ref[...] = jnp.zeros_like(ref)

    @pl.loop(0, count)
    def _(slot):
        rank = lax.rem(begin + slot, peers * work)
        block = dealing[lax.rem(rank, peers)] ^ me
        row = block * cot_rows + lax.div(rank, peers)
        ge[pl.ds(slot, 1), :] = cot_all[pl.ds(row, 1), :] * (1.0 / pixels)

    w_in_t[...] = w_in[...].astype(jnp.float32).T.astype(jnp.bfloat16)
    ga[...] = 0.5 * lax.dot_general(
        ge[...],
        w_out[...].astype(jnp.float32),
        (((1,), (1,)), ((), ())),
        precision=HIGHEST,
        preferred_element_type=jnp.float32,
    )
    starts = [
        [(y - 1 + a) * INNER_PITCH + FIRST - 1 + b for a in range(3) for b in range(3)] for y in range(1, side - 1)
    ]

    @pl.loop(0, lax.div(count + INNER_TILES - 1, INNER_TILES))
    def _(step):
        for part in range(INNER_TILES):
            slot = step * INNER_TILES + part
            base = part * (pad.shape[0] // INNER_TILES)
            for y in range(side):
                pad[pl.ds(base + y * INNER_PITCH + FIRST, side), :] = feats[slot, y].astype(jnp.float32)
        run_lines(
            step,
            INNER_TILES,
            starts,
            [True] * len(starts),
            (kern, gain[...], w_gelu, w_in_t),
            (pad, unit, invs, normed, gb, back),
            (asum, ga, tap_sum, gain_sum, gi_sum),
        )


def border_kernel(
    peers,
    work,
    parts,
    meta,
    dealing,
    links,
    own,
    inner,
    halo_pair,
    halo_cross,
    kern,
    gain,
    w_in,
    w_in_t,
    w_out,
    asum_in,
    csum,
    ge,
    ga,
    tap_in,
    gain_in,
    gi_in,
    embed_out,
    grad_out,
    pad,
    unit,
    invs,
    normed,
    gb,
    back,
    w_gelu,
    asum,
    tap_sum,
    gain_sum,
    gi_sum,
    go_sum,
    rows_out,
):
    slots, _, side, chans = own.shape
    hidden = w_in.shape[1]
    pixels = side * side
    count, begin, me, mine = meta[0], meta[1], meta[2], meta[3]
    for target, source in ((asum, asum_in), (tap_sum, tap_in), (gain_sum, gain_in), (gi_sum, gi_in)):
        target[...] = source[...]
    embed_out[...] = jnp.zeros_like(embed_out)

    split_weights(w_in, w_gelu)
    paired = lax.rem(me, 2) * -2 + 1

    def strip(column, which, slot):
        link = links[column, slot]
        index = lax.rem(jnp.maximum(link, 0), slots)
        aside = lax.div(link, slots) - me
        here, pair, cross = own[index, which], halo_pair[index, which], halo_cross[index, which]
        chosen = jnp.where(aside == 0, here, jnp.where(aside == paired, pair, cross)).astype(jnp.float32)
        return jnp.where(link >= 0, chosen, 0.0)

    lines = side + 2
    plane = lines * LINE_PITCH
    across = [a * LINE_PITCH + FIRST - 1 + b for a in range(3) for b in range(3)]
    along = [plane + b * LINE_PITCH + FIRST - 1 + a for a in range(3) for b in range(3)]
    far = (side - 1) * LINE_PITCH
    starts = [
        across,
        [start + far for start in across],
        along,
        [start + far for start in along],
    ]

    @pl.loop(0, lax.div(count + BORDER_TILES - 1, BORDER_TILES))
    def _(step):
        for part in range(BORDER_TILES):
            slot = step * BORDER_TILES + part
            rows = part * (pad.shape[0] // BORDER_TILES) + FIRST
            columns = rows + plane
            up, down, left, right = strip(0, 1, slot), strip(1, 0, slot), strip(2, 3, slot), strip(3, 2, slot)
            edge = [own[slot, i].astype(jnp.float32) for i in range(4)]
            deep = [inner[slot, i].astype(jnp.float32) for i in range(4)]
            for at, bodies, head, tail in (
                (rows, (up, edge[0], deep[0], deep[1], edge[1], down), left, right),
                (columns, (left, edge[2], deep[2], deep[3], edge[3], right), up, down),
            ):
                for line, body in zip((0, 1, 2, side - 1, side, side + 1), bodies, strict=True):
                    pad[pl.ds(at + line * LINE_PITCH, side), :] = body
                pad[pl.ds(at + LINE_PITCH - 1, side, stride=LINE_PITCH), :] = head
                pad[pl.ds(at + LINE_PITCH + side, side, stride=LINE_PITCH), :] = tail
            last = (side + 1) * LINE_PITCH
            for corner, in_rows, in_columns in (
                (strip(4, 1, slot)[side - 1 :], -1, -1),
                (strip(5, 1, slot)[:1], side, last - 1),
                (strip(6, 0, slot)[side - 1 :], last - 1, side),
                (strip(7, 0, slot)[:1], last + side, last + side),
            ):
                pad[pl.ds(rows + in_rows, 1), :] = corner
                pad[pl.ds(columns + in_columns, 1), :] = corner
        run_lines(
            step,
            BORDER_TILES,
            starts,
            [False, False, True, True],
            (kern, gain[...], w_gelu, w_in_t),
            (pad, unit, invs, normed, gb, back),
            (asum, ga, tap_sum, gain_sum, gi_sum),
        )

    asum[...] = 0.7071067811865476 * asum[...]
    go_sum[...] = lax.dot_general(
        asum[...], ge[...], (((0,), (0,)), ((), ())), precision=HIGHEST, preferred_element_type=jnp.float32
    )
    projected = jnp.dot(
        asum[...], w_out[...].astype(jnp.float32), precision=HIGHEST, preferred_element_type=jnp.float32
    )
    rows_out[...] = (csum[...] + projected) * (1.0 / pixels)

    @pl.loop(0, count)
    def _(slot):
        rank = lax.rem(begin + slot, peers * work)
        block = dealing[lax.rem(rank, peers)] ^ me
        embed_out[pl.ds(block * work + lax.div(rank, peers), 1), :] = rows_out[pl.ds(slot, 1), :]

    per = hidden // parts
    for block in range(parts):
        to = block ^ mine
        columns, offset = divmod(block * per, chans)
        grad_out[to, :per, :] = gi_sum[offset : offset + per, columns * chans : (columns + 1) * chans]
        grad_out[to, per : 2 * per, :] = go_sum[block * per : (block + 1) * per, :]
        grad_out[to, 2 * per :, :] = jnp.zeros((SMALL_ROWS, chans), jnp.float32)
    half = side // 2
    for i in range(9):
        grad_out[(i // SMALL_ROWS) ^ mine, pl.ds(2 * per + i % SMALL_ROWS, 1), :] = math.sqrt(chans) * jnp.sum(
            tap_sum[i * half : (i + 1) * half, :], axis=0, keepdims=True
        )
    grad_out[1 ^ mine, pl.ds(2 * per + 1, 1), :] = math.sqrt(chans) * (
        jnp.sum(gain_sum[...], axis=0, keepdims=True) / gain[...]
    )


def unpack_kernel(parts, meta, near, far, gk, gg, gi, go, packed):
    mine = meta[3]
    packed[: parts // 2] = near[...]
    packed[parts // 2 :] = far[...]
    hidden, chans = go.shape
    per = hidden // parts
    for block in range(parts):
        at = block ^ mine
        columns, offset = divmod(block * per, chans)
        gi[offset : offset + per, columns * chans : (columns + 1) * chans] = packed[at, :per, :]
        go[block * per : (block + 1) * per, :] = packed[at, per : 2 * per, :]
    gk[:SMALL_ROWS, :] = packed[mine, 2 * per :, :]
    gk[SMALL_ROWS:9, :] = packed[1 ^ mine, 2 * per : 2 * per + 1, :]
    gg[...] = packed[1 ^ mine, 2 * per + 1 : 2 * per + 2, :]


def local(features, tissue_count, neighbors, worker_perm, rotation, kernel, gain, w_in, w_out, cotangent):
    feats = features[0]
    slots, side, _, chans = feats.shape
    hidden = w_in.shape[1]
    cot_rows = cotangent[0]
    work = cot_rows.shape[0]
    peers = lax.axis_size("tile")
    slides = lax.axis_size("slide")
    me = lax.axis_index("tile")
    slide_bits, tile_bits = bits_of(slides), bits_of(peers)
    halving = [("slide", bit) for bit in slide_bits] + [("tile", tile_bits[0])]
    parts = 1 << len(halving)
    mine = jnp.zeros((), jnp.int32)
    for place, (axis, bit) in enumerate(reversed(halving)):
        mine = mine + jnp.where((lax.axis_index(axis) & bit) > 0, 1 << place, 0)

    feats, strips, inner, csum = border_strips(feats)
    gathered = jnp.concatenate(
        [cot_rows, jnp.broadcast_to(tissue_count.astype(jnp.float32), (8, chans))], axis=0
    )[None]
    for bit in tile_bits:
        gathered = jnp.concatenate([gathered, swap(gathered, "tile", bit)], axis=0)
        if bit == 1:
            gathered, strips = lax.optimization_barrier((gathered, strips))
            halo_pair = swap(strips, "tile", 1)
    gathered, strips = lax.optimization_barrier((gathered, strips))
    cross = [(i, i + 1) for i in range(1, peers - 1, 2)]
    halo_cross = lax.ppermute(strips, "tile", cross + [(j, i) for i, j in cross])

    counts = gathered[:, work, 0].astype(jnp.int32)
    whose = jnp.arange(peers, dtype=jnp.int32) ^ me
    begin = jnp.sum(jnp.where(whose < me, counts, 0)) + rotation[0]
    meta = jnp.stack([tissue_count[0, 0], begin, me, mine]).astype(jnp.int32)

    f32 = jnp.float32
    vmem = pl.BlockSpec(memory_space=pltpu.VMEM)
    smem = pl.BlockSpec(memory_space=pltpu.SMEM)
    shape = jax.ShapeDtypeStruct
    params = pltpu.CompilerParams(vmem_limit_bytes=VMEM_BYTES)
    gains = gain[None]
    per = hidden // parts
    block_rows = 2 * per + SMALL_ROWS

    asum, ge, ga, tap_sum, gain_sum, gi_sum, w_in_t = pl.pallas_call(
        functools.partial(inner_kernel, peers, work),
        in_specs=[smem] * 2 + [vmem] * 6,
        out_specs=[vmem] * 7,
        out_shape=[
            shape((slots, hidden), f32),
            shape((slots, chans), f32),
            shape((slots, hidden), f32),
            shape((9 * (side // 2), chans), f32),
            shape((side // 2, chans), f32),
            shape((chans, hidden), f32),
            shape((hidden, chans), jnp.bfloat16),
        ],
        scratch_shapes=line_scratch(INNER_TILES, (side + 1) * INNER_PITCH, side - 2, side, chans, hidden),
        compiler_params=params,
    )(
        meta,
        worker_perm[0],
        feats,
        gathered.reshape(peers * (work + 8), chans),
        kernel,
        gains,
        w_in,
        w_out,
    )
    embeds, packed = pl.pallas_call(
        functools.partial(border_kernel, peers, work, parts),
        in_specs=[smem] * 3 + [vmem] * 16,
        out_specs=[vmem] * 2,
        out_shape=[shape((peers * work, chans), f32), shape((parts, block_rows, chans), f32)],
        scratch_shapes=line_scratch(BORDER_TILES, 2 * (side + 2) * LINE_PITCH, 4, side, chans, hidden)
        + [
            pltpu.VMEM((slots, hidden), f32),
            pltpu.VMEM((9 * (side // 2), chans), f32),
            pltpu.VMEM((side // 2, chans), f32),
            pltpu.VMEM((chans, hidden), f32),
            pltpu.VMEM((hidden, chans), f32),
            pltpu.VMEM((slots, chans), f32),
        ],
        compiler_params=params,
    )(
        meta,
        worker_perm[0],
        neighbors[0].T,
        strips,
        inner,
        halo_pair,
        halo_cross,
        kernel,
        gains,
        w_in,
        w_in_t,
        w_out,
        asum,
        csum,
        ge,
        ga,
        tap_sum,
        gain_sum,
        gi_sum,
    )

    held = packed
    for axis, bit in halving[:-1]:
        half = held.shape[0] // 2
        held = held[:half] + swap(held[half:], axis, bit)
    embeds = embeds.reshape(peers, work, chans)
    for place, bit in enumerate(tile_bits):
        paired = embeds.reshape(embeds.shape[0] // 2, 2, work, chans)
        keep, send = paired[:, 0], paired[:, 1]
        if place == 0:
            mine_part, other_part = held[0], held[1]
        else:
            mine_part, other_part = held, held
        outgoing = jnp.concatenate([send.reshape(-1, chans), other_part], axis=0)
        incoming = swap(outgoing, "tile", bit)
        rows = send.shape[0] * work
        embeds = keep + incoming[:rows].reshape(keep.shape)
        held = mine_part + incoming[rows:]
    held = held[None]
    for axis, bit in reversed(halving[1:]):
        held = jnp.concatenate([held, swap(held, axis, bit)], axis=0)
    far = swap(held, *halving[0])
    gk, gg, gi, go = pl.pallas_call(
        functools.partial(unpack_kernel, parts),
        in_specs=[smem, vmem, vmem],
        out_specs=[vmem] * 4,
        out_shape=[
            jax.ShapeDtypeStruct((9, chans), f32),
            jax.ShapeDtypeStruct((1, chans), f32),
            jax.ShapeDtypeStruct((chans, hidden), f32),
            jax.ShapeDtypeStruct((hidden, chans), f32),
        ],
        scratch_shapes=[pltpu.VMEM((parts, block_rows, chans), f32)],
        compiler_params=params,
    )(meta, held, far)
    return embeds, gk, gg[0], gi, go


def solution(mesh):
    placed = (
        P("slide", "tile", None, None, None),
        P("slide", "tile"),
        P("slide", "tile", None),
        P("slide", None),
        P("slide"),
        P(),
        P(),
        P(),
        P(),
        P("slide", "tile", None),
    )
    return jax.shard_map(
        local,
        mesh=mesh,
        in_specs=placed,
        out_specs=(P("slide", "tile", None), P(), P(), P(), P()),
        check_vma=False,
    )
```

```python
import functools
import math

import jax
import jax.numpy as jnp
from jax import lax
from jax.experimental import pallas as pl
from jax.experimental.pallas import tpu as pltpu
from jax.sharding import PartitionSpec as P

HIGHEST = lax.Precision.HIGHEST
FIRST = 8
INNER_PITCH = 24
LINE_PITCH = 32
INNER_TILES = 4
BORDER_TILES = 16
SMALL_ROWS = 8
STRIP_TILES = 4
VMEM_BYTES = 32 * 1024 * 1024
INNER_BYTES = 53 * 1024 * 1024


def bits_of(count):
    return [1 << bit for bit in range(count.bit_length() - 1)]


def swap(value, axis, bit):
    count = lax.axis_size(axis)
    return lax.ppermute(value, axis, [(i, i ^ bit) for i in range(count)])


def strip_kernel(tiles, strips, inner, csum):
    slots, side, _, chans = tiles.shape
    columns = (0, side - 1, 1, side - 2)
    rows = (len(columns) + 1) * side
    row = lax.broadcasted_iota(jnp.int32, (rows, side * side), 0)
    pixel = lax.broadcasted_iota(jnp.int32, (rows, side * side), 1)
    group = lax.div(row, side)
    column = jnp.where(group == 0, columns[0], jnp.where(group == 1, columns[1], jnp.where(group == 2, columns[2], columns[3])))
    picked = (pixel == (row - group * side) * side + column) | (group == len(columns))
    select = jnp.where(picked, 1.0, 0.0).astype(jnp.bfloat16)

    @pl.loop(0, slots // STRIP_TILES)
    def _(step):
        for part in range(STRIP_TILES):
            slot = step * STRIP_TILES + part
            tile = tiles[slot].reshape(side * side, chans)
            found = jnp.dot(select, tile, preferred_element_type=jnp.float32)
            lines = found[: len(columns) * side].astype(jnp.bfloat16)
            strips[slot, 0] = tiles[slot, 0]
            strips[slot, 1] = tiles[slot, side - 1]
            strips[slot, 2] = lines[:side]
            strips[slot, 3] = lines[side : 2 * side]
            inner[slot, 0] = tiles[slot, 1]
            inner[slot, 1] = tiles[slot, side - 2]
            inner[slot, 2] = lines[2 * side : 3 * side]
            inner[slot, 3] = lines[3 * side :]
            csum[pl.ds(slot, 1), :] = found[len(columns) * side : len(columns) * side + 1]


def border_strips(tiles):
    slots, side, _, chans = tiles.shape
    shape = jax.ShapeDtypeStruct((slots, 4, side, chans), jnp.bfloat16)
    spec = pl.BlockSpec(memory_space=pltpu.VMEM)
    return pl.pallas_call(
        strip_kernel,
        in_specs=[spec],
        out_specs=[spec] * 3,
        out_shape=[shape, shape, jax.ShapeDtypeStruct((slots, chans), jnp.float32)],
        compiler_params=pltpu.CompilerParams(vmem_limit_bytes=VMEM_BYTES),
        cost_estimate=pl.CostEstimate(flops=10**9, bytes_accessed=10**7, transcendentals=0),
    )(tiles)


def spread(rows, lines):
    return rows.reshape(lines, rows.shape[0] // lines, rows.shape[1])


def run_lines(
    step, tiles, starts, masked, weights, state, sums
):
    kern, gains, w_gelu, w_in_t = weights
    pad, unit, invs, normed, gb, back = state
    asum, ga, tap_sum, gain_sum, gi_sum = sums
    lines = len(starts)
    pad_rows = pad.shape[0] // tiles
    pixels = normed.shape[0] // tiles
    side = pixels // lines
    hidden, chans = w_in_t.shape
    half = side // 2
    gains_root = gains * math.sqrt(chans)
    wide_taps = kern[...].astype(jnp.float32)
    taps = [jnp.broadcast_to(wide_taps[i : i + 1, :], (side, chans)) for i in range(9)]
    place = lax.broadcasted_iota(jnp.int32, (side, hidden), 0)
    inside = jnp.where((place > 0) & (place < side - 1), 1.0, 0.0)
    for part in range(tiles):
        base = part * pad_rows
        for line in range(lines):
            depth = None
            for tap in range(9):
                term = pad[pl.ds(base + starts[line][tap], side), :] * taps[tap]
                depth = term if depth is None else depth + term
            centered = depth - jnp.mean(depth, axis=1, keepdims=True)
            inverse = lax.rsqrt(jnp.sum(centered * centered, axis=1, keepdims=True) + chans * 1e-06)
            units = centered * inverse
            at = part * pixels + line * side
            unit[at : at + side, :] = units
            invs[at : at + side, :] = jnp.broadcast_to(inverse, (side, chans))
            normed[at : at + side, :] = (units * gains_root).astype(jnp.bfloat16)
    for part in range(tiles):
        slot = step * tiles + part
        rows = slice(part * pixels, (part + 1) * pixels)
        doubled = jnp.concatenate([normed[rows, :]] * 2, axis=1)
        scaled = jnp.dot(doubled, w_gelu[...], preferred_element_type=jnp.float32)
        twice = 1.0 + lax.erf(scaled)
        bell = jnp.exp2(scaled * scaled * -1.4426950408889634)
        act = spread(scaled * twice, lines)
        slope = spread(twice + (scaled * 1.1283791670955126) * bell, lines)
        factor = jnp.broadcast_to(ga[pl.ds(slot, 1), :], (side, hidden))
        factor_inside = factor * inside
        whole = [act[line] for line in range(lines) if not masked[line]]
        partial = [act[line] for line in range(lines) if masked[line]]
        total = functools.reduce(jnp.add, partial) * inside
        if whole:
            total = total + functools.reduce(jnp.add, whole)
        asum[pl.ds(slot, 1), :] += jnp.sum(total, axis=0, keepdims=True)
        for line in range(lines):
            at = part * pixels + line * side
            gb[at : at + side, :] = (slope[line] * (factor_inside if masked[line] else factor)).astype(jnp.bfloat16)
    back[...] = jnp.dot(gb[...], w_in_t[...], preferred_element_type=jnp.float32)
    gi_sum[...] += lax.dot_general(normed[...], gb[...], (((0,), (0,)), ((), ())), preferred_element_type=jnp.float32)
    gain_part = jnp.zeros((half, chans), jnp.float32)
    tap_part = [jnp.zeros((half, chans), jnp.float32) for _ in range(9)]
    for part in range(tiles):
        base = part * pad_rows
        for line in range(lines):
            at = part * pixels + line * side
            units = unit[at : at + side, :]
            grad_unit = back[at : at + side, :] * gains
            product = grad_unit * units
            gain_part = gain_part + (product[:half] + product[half:])
            grad_depth = invs[at : at + side, :] * (
                grad_unit
                - jnp.mean(grad_unit, axis=1, keepdims=True)
                - units * jnp.sum(product, axis=1, keepdims=True)
            )
            for tap in range(9):
                term = grad_depth * pad[pl.ds(base + starts[line][tap], side), :]
                tap_part[tap] = tap_part[tap] + (term[:half] + term[half:])
    gain_sum[...] += gain_part
    for tap in range(9):
        tap_sum[tap * half : (tap + 1) * half, :] += tap_part[tap]


def line_scratch(tiles, pad_rows, lines, side, chans, hidden):
    f32, bf16 = jnp.float32, jnp.bfloat16
    pixels = tiles * lines * side
    return [
        pltpu.VMEM((tiles * pad_rows, chans), f32),
        pltpu.VMEM((pixels, chans), f32),
        pltpu.VMEM((pixels, chans), f32),
        pltpu.VMEM((pixels, chans), bf16),
        pltpu.VMEM((pixels, hidden), bf16),
        pltpu.VMEM((pixels, chans), f32),
        pltpu.VMEM((2 * chans, hidden), bf16),
    ]


def split_weights(w_in, w_gelu):
    chans = w_in.shape[0]
    scaled = w_in[...].astype(jnp.float32) * 0.7071067811865476
    high = scaled.astype(jnp.bfloat16)
    w_gelu[:chans, :] = high
    w_gelu[chans:, :] = (scaled - high.astype(jnp.float32)).astype(jnp.bfloat16)


def inner_kernel(
    peers,
    work,
    meta,
    dealing,
    feats_hbm,
    cot_near,
    cot_far,
    kern,
    gain,
    w_in,
    w_out_hbm,
    asum,
    ge,
    ga,
    tap_sum,
    gain_sum,
    gi_sum,
    w_in_t,
    begin_out,
    pad,
    unit,
    invs,
    normed,
    gb,
    back,
    w_gelu,
    feats,
    w_out,
    cot_all,
    tile_sems,
    weight_sem,
):
    side = feats.shape[1]
    chans = feats.shape[3]
    pixels = side * side
    cot_rows = cot_all.shape[0] // peers
    count, turned, me = meta[0], meta[1], meta[2]
    steps = lax.div(count + INNER_TILES - 1, INNER_TILES)

    def tiles_copy(step):
        taken = pl.ds(step * INNER_TILES, INNER_TILES)
        return pltpu.make_async_copy(feats_hbm.at[taken], feats.at[taken], tile_sems.at[step])

    weight_copy = pltpu.make_async_copy(w_out_hbm, w_out, weight_sem)
    weight_copy.start()

    @pl.loop(0, steps)
    def _(step):
        tiles_copy(step).start()

    half_rows = cot_near.shape[0]
    cot_all[:half_rows, :] = cot_near[...]
    cot_all[half_rows:, :] = cot_far[...]
    counts = cot_all[pl.ds(work, peers, stride=cot_rows), :]
    whose = lax.broadcasted_iota(jnp.int32, counts.shape, 0) ^ me
    lane = lax.broadcasted_iota(jnp.int32, counts.shape, 1)
    begin = turned + jnp.sum(jnp.where((whose < me) & (lane == 0), counts, 0.0)).astype(jnp.int32)
    begin_out[0] = begin
    split_weights(w_in, w_gelu)
    for ref in (asum, ge, tap_sum, gain_sum, gi_sum, pad):
        ref[...] = jnp.zeros_like(ref)

    @pl.loop(0, count)
    def _(slot):
        rank = lax.rem(begin + slot, peers * work)
        block = dealing[lax.rem(rank, peers)] ^ me
        row = block * cot_rows + lax.div(rank, peers)
        ge[pl.ds(slot, 1), :] = cot_all[pl.ds(row, 1), :] * (1.0 / pixels)

    w_in_t[...] = w_in[...].astype(jnp.float32).T.astype(jnp.bfloat16)
    weight_copy.wait()
    ga[...] = 0.5 * lax.dot_general(
        ge[...],
        w_out[...].astype(jnp.float32),
        (((1,), (1,)), ((), ())),
        precision=HIGHEST,
        preferred_element_type=jnp.float32,
    )
    starts = [
        [(y - 1 + a) * INNER_PITCH + FIRST - 1 + b for a in range(3) for b in range(3)] for y in range(1, side - 1)
    ]

    @pl.loop(0, steps)
    def _(step):
        tiles_copy(step).wait()
        for part in range(INNER_TILES):
            slot = step * INNER_TILES + part
            base = part * (pad.shape[0] // INNER_TILES)
            for y in range(side):
                pad[pl.ds(base + y * INNER_PITCH + FIRST, side), :] = feats[slot, y].astype(jnp.float32)
        run_lines(
            step,
            INNER_TILES,
            starts,
            [True] * len(starts),
            (kern, gain[...], w_gelu, w_in_t),
            (pad, unit, invs, normed, gb, back),
            (asum, ga, tap_sum, gain_sum, gi_sum),
        )


def border_kernel(
    peers,
    work,
    parts,
    meta,
    begin_in,
    dealing,
    links,
    own,
    inner,
    halo_pair,
    halo_cross,
    kern,
    gain,
    w_in,
    w_in_t,
    w_out,
    asum_in,
    csum,
    ge,
    ga,
    tap_in,
    gain_in,
    gi_in,
    embed_out,
    grad_out,
    pad,
    unit,
    invs,
    normed,
    gb,
    back,
    w_gelu,
    asum,
    tap_sum,
    gain_sum,
    gi_sum,
    go_sum,
    rows_out,
):
    slots, _, side, chans = own.shape
    hidden = w_in.shape[1]
    pixels = side * side
    count, begin, me, mine = meta[0], begin_in[0], meta[2], meta[3]
    for target, source in ((asum, asum_in), (tap_sum, tap_in), (gain_sum, gain_in), (gi_sum, gi_in)):
        target[...] = source[...]
    embed_out[...] = jnp.zeros_like(embed_out)

    split_weights(w_in, w_gelu)
    paired = lax.rem(me, 2) * -2 + 1

    def strip(column, which, slot):
        link = links[column, slot]
        index = lax.rem(jnp.maximum(link, 0), slots)
        aside = lax.div(link, slots) - me
        here, pair, cross = own[index, which], halo_pair[index, which], halo_cross[index, which]
        chosen = jnp.where(aside == 0, here, jnp.where(aside == paired, pair, cross)).astype(jnp.float32)
        return jnp.where(link >= 0, chosen, 0.0)

    lines = side + 2
    plane = lines * LINE_PITCH
    across = [a * LINE_PITCH + FIRST - 1 + b for a in range(3) for b in range(3)]
    along = [plane + b * LINE_PITCH + FIRST - 1 + a for a in range(3) for b in range(3)]
    far = (side - 1) * LINE_PITCH
    starts = [
        across,
        [start + far for start in across],
        along,
        [start + far for start in along],
    ]

    @pl.loop(0, lax.div(count + BORDER_TILES - 1, BORDER_TILES))
    def _(step):
        for part in range(BORDER_TILES):
            slot = step * BORDER_TILES + part
            rows = part * (pad.shape[0] // BORDER_TILES) + FIRST
            columns = rows + plane
            up, down, left, right = strip(0, 1, slot), strip(1, 0, slot), strip(2, 3, slot), strip(3, 2, slot)
            edge = [own[slot, i].astype(jnp.float32) for i in range(4)]
            deep = [inner[slot, i].astype(jnp.float32) for i in range(4)]
            for at, bodies, head, tail in (
                (rows, (up, edge[0], deep[0], deep[1], edge[1], down), left, right),
                (columns, (left, edge[2], deep[2], deep[3], edge[3], right), up, down),
            ):
                for line, body in zip((0, 1, 2, side - 1, side, side + 1), bodies, strict=True):
                    pad[pl.ds(at + line * LINE_PITCH, side), :] = body
                pad[pl.ds(at + LINE_PITCH - 1, side, stride=LINE_PITCH), :] = head
                pad[pl.ds(at + LINE_PITCH + side, side, stride=LINE_PITCH), :] = tail
            last = (side + 1) * LINE_PITCH
            for corner, in_rows, in_columns in (
                (strip(4, 1, slot)[side - 1 :], -1, -1),
                (strip(5, 1, slot)[:1], side, last - 1),
                (strip(6, 0, slot)[side - 1 :], last - 1, side),
                (strip(7, 0, slot)[:1], last + side, last + side),
            ):
                pad[pl.ds(rows + in_rows, 1), :] = corner
                pad[pl.ds(columns + in_columns, 1), :] = corner
        run_lines(
            step,
            BORDER_TILES,
            starts,
            [False, False, True, True],
            (kern, gain[...], w_gelu, w_in_t),
            (pad, unit, invs, normed, gb, back),
            (asum, ga, tap_sum, gain_sum, gi_sum),
        )

    asum[...] = 0.7071067811865476 * asum[...]
    go_sum[...] = lax.dot_general(
        asum[...], ge[...], (((0,), (0,)), ((), ())), precision=HIGHEST, preferred_element_type=jnp.float32
    )
    projected = jnp.dot(
        asum[...], w_out[...].astype(jnp.float32), precision=HIGHEST, preferred_element_type=jnp.float32
    )
    rows_out[...] = (csum[...] + projected) * (1.0 / pixels)

    @pl.loop(0, count)
    def _(slot):
        rank = lax.rem(begin + slot, peers * work)
        block = dealing[lax.rem(rank, peers)] ^ me
        embed_out[pl.ds(block * work + lax.div(rank, peers), 1), :] = rows_out[pl.ds(slot, 1), :]

    per = hidden // parts
    for block in range(parts):
        to = block ^ mine
        columns, offset = divmod(block * per, chans)
        grad_out[to, :per, :] = gi_sum[offset : offset + per, columns * chans : (columns + 1) * chans]
        grad_out[to, per : 2 * per, :] = go_sum[block * per : (block + 1) * per, :]
        grad_out[to, 2 * per :, :] = jnp.zeros((SMALL_ROWS, chans), jnp.float32)
    half = side // 2
    for i in range(9):
        grad_out[(i // SMALL_ROWS) ^ mine, pl.ds(2 * per + i % SMALL_ROWS, 1), :] = math.sqrt(chans) * jnp.sum(
            tap_sum[i * half : (i + 1) * half, :], axis=0, keepdims=True
        )
    grad_out[1 ^ mine, pl.ds(2 * per + 1, 1), :] = math.sqrt(chans) * (
        jnp.sum(gain_sum[...], axis=0, keepdims=True) / gain[...]
    )


def unpack_kernel(parts, meta, near, far, gk, gg, gi, go, packed):
    mine = meta[3]
    packed[: parts // 2] = near[...]
    packed[parts // 2 :] = far[...]
    hidden, chans = go.shape
    per = hidden // parts
    for block in range(parts):
        at = block ^ mine
        columns, offset = divmod(block * per, chans)
        gi[offset : offset + per, columns * chans : (columns + 1) * chans] = packed[at, :per, :]
        go[block * per : (block + 1) * per, :] = packed[at, per : 2 * per, :]
    gk[:SMALL_ROWS, :] = packed[mine, 2 * per :, :]
    gk[SMALL_ROWS:9, :] = packed[1 ^ mine, 2 * per : 2 * per + 1, :]
    gg[...] = packed[1 ^ mine, 2 * per + 1 : 2 * per + 2, :]


def local(features, tissue_count, neighbors, worker_perm, rotation, kernel, gain, w_in, w_out, cotangent):
    feats = features[0]
    slots, side, _, chans = feats.shape
    hidden = w_in.shape[1]
    cot_rows = cotangent[0]
    work = cot_rows.shape[0]
    peers = lax.axis_size("tile")
    slides = lax.axis_size("slide")
    me = lax.axis_index("tile")
    slide_bits, tile_bits = bits_of(slides), bits_of(peers)
    halving = [("slide", bit) for bit in slide_bits] + [("tile", tile_bits[0])]
    parts = 1 << len(halving)
    mine = jnp.zeros((), jnp.int32)
    for place, (axis, bit) in enumerate(reversed(halving)):
        mine = mine + jnp.where((lax.axis_index(axis) & bit) > 0, 1 << place, 0)

    strips, inner, csum = border_strips(feats)
    gathered = jnp.concatenate(
        [cot_rows, jnp.broadcast_to(tissue_count.astype(jnp.float32), (8, chans))], axis=0
    )[None]
    for bit in tile_bits:
        arrived = swap(gathered, "tile", bit)
        if bit == tile_bits[0]:
            arrived, strips = lax.optimization_barrier((arrived, strips))
            halo_pair = swap(strips, "tile", 1)
        if bit < tile_bits[-1]:
            gathered = jnp.concatenate([gathered, arrived], axis=0)
    arrived, strips = lax.optimization_barrier((arrived, strips))
    cross = [(i, i + 1) for i in range(1, peers - 1, 2)]
    halo_cross = lax.ppermute(strips, "tile", cross + [(j, i) for i, j in cross])
    meta = jnp.stack([tissue_count[0, 0], rotation[0], me, mine]).astype(jnp.int32)

    f32 = jnp.float32
    vmem = pl.BlockSpec(memory_space=pltpu.VMEM)
    smem = pl.BlockSpec(memory_space=pltpu.SMEM)
    shape = jax.ShapeDtypeStruct
    params = pltpu.CompilerParams(vmem_limit_bytes=VMEM_BYTES)
    inner_params = pltpu.CompilerParams(vmem_limit_bytes=INNER_BYTES)
    gains = gain[None]
    per = hidden // parts
    block_rows = 2 * per + SMALL_ROWS

    far_space = pl.BlockSpec(memory_space=pltpu.HBM)
    near_rows = peers // 2 * (work + 8)
    asum, ge, ga, tap_sum, gain_sum, gi_sum, w_in_t, begin = pl.pallas_call(
        functools.partial(inner_kernel, peers, work),
        in_specs=[smem] * 2 + [far_space] + [vmem] * 5 + [far_space],
        out_specs=[vmem] * 7 + [smem],
        out_shape=[
            shape((slots, hidden), f32),
            shape((slots, chans), f32),
            shape((slots, hidden), f32),
            shape((9 * (side // 2), chans), f32),
            shape((side // 2, chans), f32),
            shape((chans, hidden), f32),
            shape((hidden, chans), jnp.bfloat16),
            shape((1,), jnp.int32),
        ],
        scratch_shapes=line_scratch(INNER_TILES, (side + 1) * INNER_PITCH, side - 2, side, chans, hidden)
        + [
            pltpu.VMEM(feats.shape, jnp.bfloat16),
            pltpu.VMEM((hidden, chans), jnp.bfloat16),
            pltpu.VMEM((2 * near_rows, chans), f32),
            pltpu.SemaphoreType.DMA((slots // INNER_TILES,)),
            pltpu.SemaphoreType.DMA,
        ],
        compiler_params=inner_params,
    )(
        meta,
        worker_perm[0],
        feats,
        gathered.reshape(near_rows, chans),
        arrived.reshape(near_rows, chans),
        kernel,
        gains,
        w_in,
        w_out,
    )
    embeds, packed = pl.pallas_call(
        functools.partial(border_kernel, peers, work, parts),
        in_specs=[smem] * 4 + [vmem] * 16,
        out_specs=[vmem] * 2,
        out_shape=[shape((peers * work, chans), f32), shape((parts, block_rows, chans), f32)],
        scratch_shapes=line_scratch(BORDER_TILES, 2 * (side + 2) * LINE_PITCH, 4, side, chans, hidden)
        + [
            pltpu.VMEM((slots, hidden), f32),
            pltpu.VMEM((9 * (side // 2), chans), f32),
            pltpu.VMEM((side // 2, chans), f32),
            pltpu.VMEM((chans, hidden), f32),
            pltpu.VMEM((hidden, chans), f32),
            pltpu.VMEM((slots, chans), f32),
        ],
        compiler_params=params,
    )(
        meta,
        begin,
        worker_perm[0],
        neighbors[0].T,
        strips,
        inner,
        halo_pair,
        halo_cross,
        kernel,
        gains,
        w_in,
        w_in_t,
        w_out,
        asum,
        csum,
        ge,
        ga,
        tap_sum,
        gain_sum,
        gi_sum,
    )

    held = packed
    for axis, bit in halving[:-1]:
        half = held.shape[0] // 2
        held = held[:half] + swap(held[half:], axis, bit)
    embeds = embeds.reshape(peers, work, chans)
    for place, bit in enumerate(tile_bits):
        paired = embeds.reshape(embeds.shape[0] // 2, 2, work, chans)
        keep, send = paired[:, 0], paired[:, 1]
        if place == 0:
            mine_part, other_part = held[0], held[1]
        else:
            mine_part, other_part = held, held
        outgoing = jnp.concatenate([send.reshape(-1, chans), other_part], axis=0)
        incoming = swap(outgoing, "tile", bit)
        rows = send.shape[0] * work
        embeds = keep + incoming[:rows].reshape(keep.shape)
        held = mine_part + incoming[rows:]
    held = held[None]
    for axis, bit in reversed(halving[1:]):
        held = jnp.concatenate([held, swap(held, axis, bit)], axis=0)
    far = swap(held, *halving[0])
    gk, gg, gi, go = pl.pallas_call(
        functools.partial(unpack_kernel, parts),
        in_specs=[smem, vmem, vmem],
        out_specs=[vmem] * 4,
        out_shape=[
            jax.ShapeDtypeStruct((9, chans), f32),
            jax.ShapeDtypeStruct((1, chans), f32),
            jax.ShapeDtypeStruct((chans, hidden), f32),
            jax.ShapeDtypeStruct((hidden, chans), f32),
        ],
        scratch_shapes=[pltpu.VMEM((parts, block_rows, chans), f32)],
        compiler_params=params,
    )(meta, held, far)
    return embeds, gk, gg[0], gi, go


def solution(mesh):
    placed = (
        P("slide", "tile", None, None, None),
        P("slide", "tile"),
        P("slide", "tile", None),
        P("slide", None),
        P("slide"),
        P(),
        P(),
        P(),
        P(),
        P("slide", "tile", None),
    )
    return jax.shard_map(
        local,
        mesh=mesh,
        in_specs=placed,
        out_specs=(P("slide", "tile", None), P(), P(), P(), P()),
        check_vma=False,
    )
```

```python
import functools
import math

import jax
import jax.numpy as jnp
from jax import lax
from jax.experimental import pallas as pl
from jax.experimental.pallas import tpu as pltpu
from jax.sharding import PartitionSpec as P

HIGHEST = lax.Precision.HIGHEST
FIRST = 8
INNER_PITCH = 24
LINE_PITCH = 32
INNER_TILES = 4
BORDER_TILES = 16
SMALL_ROWS = 8
STRIP_TILES = 8
VMEM_BYTES = 32 * 1024 * 1024
STRIP_BYTES = 54 * 1024 * 1024
INNER_BYTES = 48 * 1024 * 1024


def bits_of(count):
    return [1 << bit for bit in range(count.bit_length() - 1)]


def swap(value, axis, bit):
    count = lax.axis_size(axis)
    return lax.ppermute(value, axis, [(i, i ^ bit) for i in range(count)])


def strip_kernel(tiles_hbm, strips, inner, csum, tiles, sems):
    slots, side, _, chans = tiles_hbm.shape
    columns = (0, side - 1, 1, side - 2)
    rows = (len(columns) + 1) * side
    row = lax.broadcasted_iota(jnp.int32, (rows, side * side), 0)
    pixel = lax.broadcasted_iota(jnp.int32, (rows, side * side), 1)
    group = lax.div(row, side)
    column = jnp.where(group == 0, columns[0], jnp.where(group == 1, columns[1], jnp.where(group == 2, columns[2], columns[3])))
    picked = (pixel == (row - group * side) * side + column) | (group == len(columns))
    select = jnp.where(picked, 1.0, 0.0).astype(jnp.bfloat16)

    def tiles_copy(step):
        taken = pl.ds(step * STRIP_TILES, STRIP_TILES)
        return pltpu.make_async_copy(tiles_hbm.at[taken], tiles.at[taken], sems.at[step])

    @pl.loop(0, slots // STRIP_TILES)
    def _(step):
        tiles_copy(step).start()

    @pl.loop(0, slots // STRIP_TILES)
    def _(step):
        tiles_copy(step).wait()
        for part in range(STRIP_TILES):
            slot = step * STRIP_TILES + part
            tile = tiles[slot].reshape(side * side, chans)
            found = jnp.dot(select, tile, preferred_element_type=jnp.float32)
            lines = found[: len(columns) * side].astype(jnp.bfloat16)
            strips[slot, 0] = tiles[slot, 0]
            strips[slot, 1] = tiles[slot, side - 1]
            strips[slot, 2] = lines[:side]
            strips[slot, 3] = lines[side : 2 * side]
            inner[slot, 0] = tiles[slot, 1]
            inner[slot, 1] = tiles[slot, side - 2]
            inner[slot, 2] = lines[2 * side : 3 * side]
            inner[slot, 3] = lines[3 * side :]
            csum[pl.ds(slot, 1), :] = found[len(columns) * side : len(columns) * side + 1]


def border_strips(tiles):
    slots, side, _, chans = tiles.shape
    shape = jax.ShapeDtypeStruct((slots, 4, side, chans), jnp.bfloat16)
    spec = pl.BlockSpec(memory_space=pltpu.VMEM)
    return pl.pallas_call(
        strip_kernel,
        in_specs=[pl.BlockSpec(memory_space=pltpu.HBM)],
        out_specs=[spec] * 3,
        out_shape=[shape, shape, jax.ShapeDtypeStruct((slots, chans), jnp.float32)],
        scratch_shapes=[
            pltpu.VMEM(tiles.shape, jnp.bfloat16),
            pltpu.SemaphoreType.DMA((slots // STRIP_TILES,)),
        ],
        compiler_params=pltpu.CompilerParams(vmem_limit_bytes=STRIP_BYTES),
    )(tiles)


def spread(rows, lines):
    return rows.reshape(lines, rows.shape[0] // lines, rows.shape[1])


def run_lines(
    step, tiles, starts, masked, weights, state, sums
):
    kern, gains, w_gelu, w_in_t = weights
    pad, unit, invs, normed, gb, back = state
    asum, ga, tap_sum, gain_sum, gi_sum = sums
    lines = len(starts)
    pad_rows = pad.shape[0] // tiles
    pixels = normed.shape[0] // tiles
    side = pixels // lines
    hidden, chans = w_in_t.shape
    half = side // 2
    gains_root = gains * math.sqrt(chans)
    wide_taps = kern[...].astype(jnp.float32)
    taps = [jnp.broadcast_to(wide_taps[i : i + 1, :], (side, chans)) for i in range(9)]
    place = lax.broadcasted_iota(jnp.int32, (side, hidden), 0)
    inside = jnp.where((place > 0) & (place < side - 1), 1.0, 0.0)
    for part in range(tiles):
        base = part * pad_rows
        for line in range(lines):
            depth = None
            for tap in range(9):
                term = pad[pl.ds(base + starts[line][tap], side), :] * taps[tap]
                depth = term if depth is None else depth + term
            centered = depth - jnp.mean(depth, axis=1, keepdims=True)
            inverse = lax.rsqrt(jnp.sum(centered * centered, axis=1, keepdims=True) + chans * 1e-06)
            units = centered * inverse
            at = part * pixels + line * side
            unit[at : at + side, :] = units
            invs[at : at + side, :] = jnp.broadcast_to(inverse, (side, chans))
            normed[at : at + side, :] = (units * gains_root).astype(jnp.bfloat16)
    for part in range(tiles):
        slot = step * tiles + part
        rows = slice(part * pixels, (part + 1) * pixels)
        doubled = jnp.concatenate([normed[rows, :]] * 2, axis=1)
        scaled = jnp.dot(doubled, w_gelu[...], preferred_element_type=jnp.float32)
        twice = 1.0 + lax.erf(scaled)
        bell = jnp.exp2(scaled * scaled * -1.4426950408889634)
        act = spread(scaled * twice, lines)
        slope = spread(twice + (scaled * 1.1283791670955126) * bell, lines)
        factor = jnp.broadcast_to(ga[pl.ds(slot, 1), :], (side, hidden))
        factor_inside = factor * inside
        whole = [act[line] for line in range(lines) if not masked[line]]
        partial = [act[line] for line in range(lines) if masked[line]]
        total = functools.reduce(jnp.add, partial) * inside
        if whole:
            total = total + functools.reduce(jnp.add, whole)
        asum[pl.ds(slot, 1), :] += jnp.sum(total, axis=0, keepdims=True)
        for line in range(lines):
            at = part * pixels + line * side
            gb[at : at + side, :] = (slope[line] * (factor_inside if masked[line] else factor)).astype(jnp.bfloat16)
    back[...] = jnp.dot(gb[...], w_in_t[...], preferred_element_type=jnp.float32)
    gi_sum[...] += lax.dot_general(normed[...], gb[...], (((0,), (0,)), ((), ())), preferred_element_type=jnp.float32)
    gain_part = jnp.zeros((half, chans), jnp.float32)
    tap_part = [jnp.zeros((half, chans), jnp.float32) for _ in range(9)]
    for part in range(tiles):
        base = part * pad_rows
        for line in range(lines):
            at = part * pixels + line * side
            units = unit[at : at + side, :]
            grad_unit = back[at : at + side, :] * gains
            product = grad_unit * units
            gain_part = gain_part + (product[:half] + product[half:])
            grad_depth = invs[at : at + side, :] * (
                grad_unit
                - jnp.mean(grad_unit, axis=1, keepdims=True)
                - units * jnp.sum(product, axis=1, keepdims=True)
            )
            for tap in range(9):
                term = grad_depth * pad[pl.ds(base + starts[line][tap], side), :]
                tap_part[tap] = tap_part[tap] + (term[:half] + term[half:])
    gain_sum[...] += gain_part
    for tap in range(9):
        tap_sum[tap * half : (tap + 1) * half, :] += tap_part[tap]


def line_scratch(tiles, pad_rows, lines, side, chans, hidden):
    f32, bf16 = jnp.float32, jnp.bfloat16
    pixels = tiles * lines * side
    return [
        pltpu.VMEM((tiles * pad_rows, chans), f32),
        pltpu.VMEM((pixels, chans), f32),
        pltpu.VMEM((pixels, chans), f32),
        pltpu.VMEM((pixels, chans), bf16),
        pltpu.VMEM((pixels, hidden), bf16),
        pltpu.VMEM((pixels, chans), f32),
        pltpu.VMEM((2 * chans, hidden), bf16),
    ]


def split_weights(w_in, w_gelu):
    chans = w_in.shape[0]
    scaled = w_in[...].astype(jnp.float32) * 0.7071067811865476
    high = scaled.astype(jnp.bfloat16)
    w_gelu[:chans, :] = high
    w_gelu[chans:, :] = (scaled - high.astype(jnp.float32)).astype(jnp.bfloat16)


def inner_kernel(
    peers,
    work,
    meta,
    dealing,
    feats_hbm,
    cot_near,
    cot_far,
    kern,
    gain,
    w_in,
    w_out_hbm,
    asum,
    ge,
    ga,
    tap_sum,
    gain_sum,
    gi_sum,
    w_in_t,
    begin_out,
    pad,
    unit,
    invs,
    normed,
    gb,
    back,
    w_gelu,
    feats,
    w_out,
    cot_all,
    tile_sems,
    weight_sem,
):
    side = feats.shape[1]
    chans = feats.shape[3]
    pixels = side * side
    cot_rows = cot_all.shape[0] // peers
    count, turned, me = meta[0], meta[1], meta[2]
    steps = lax.div(count + INNER_TILES - 1, INNER_TILES)

    def tiles_copy(step):
        taken = pl.ds(step * INNER_TILES, INNER_TILES)
        return pltpu.make_async_copy(feats_hbm.at[taken], feats.at[taken], tile_sems.at[step])

    weight_copy = pltpu.make_async_copy(w_out_hbm, w_out, weight_sem)
    weight_copy.start()

    @pl.loop(0, steps)
    def _(step):
        tiles_copy(step).start()

    half_rows = cot_near.shape[0]
    cot_all[:half_rows, :] = cot_near[...]
    cot_all[half_rows:, :] = cot_far[...]
    counts = cot_all[pl.ds(work, peers, stride=cot_rows), :]
    whose = lax.broadcasted_iota(jnp.int32, counts.shape, 0) ^ me
    lane = lax.broadcasted_iota(jnp.int32, counts.shape, 1)
    begin = turned + jnp.sum(jnp.where((whose < me) & (lane == 0), counts, 0.0)).astype(jnp.int32)
    begin_out[0] = begin
    split_weights(w_in, w_gelu)
    for ref in (asum, ge, tap_sum, gain_sum, gi_sum, pad):
        ref[...] = jnp.zeros_like(ref)

    @pl.loop(0, count)
    def _(slot):
        rank = lax.rem(begin + slot, peers * work)
        block = dealing[lax.rem(rank, peers)] ^ me
        row = block * cot_rows + lax.div(rank, peers)
        ge[pl.ds(slot, 1), :] = cot_all[pl.ds(row, 1), :] * (1.0 / pixels)

    w_in_t[...] = w_in[...].astype(jnp.float32).T.astype(jnp.bfloat16)
    weight_copy.wait()
    ga[...] = 0.5 * lax.dot_general(
        ge[...],
        w_out[...].astype(jnp.float32),
        (((1,), (1,)), ((), ())),
        precision=HIGHEST,
        preferred_element_type=jnp.float32,
    )
    starts = [
        [(y - 1 + a) * INNER_PITCH + FIRST - 1 + b for a in range(3) for b in range(3)] for y in range(1, side - 1)
    ]

    @pl.loop(0, steps)
    def _(step):
        tiles_copy(step).wait()
        for part in range(INNER_TILES):
            slot = step * INNER_TILES + part
            base = part * (pad.shape[0] // INNER_TILES)
            for y in range(side):
                pad[pl.ds(base + y * INNER_PITCH + FIRST, side), :] = feats[slot, y].astype(jnp.float32)
        run_lines(
            step,
            INNER_TILES,
            starts,
            [True] * len(starts),
            (kern, gain[...], w_gelu, w_in_t),
            (pad, unit, invs, normed, gb, back),
            (asum, ga, tap_sum, gain_sum, gi_sum),
        )


def border_kernel(
    peers,
    work,
    parts,
    meta,
    begin_in,
    dealing,
    links,
    own,
    inner,
    halo_pair,
    halo_cross,
    kern,
    gain,
    w_in,
    w_in_t,
    w_out,
    asum_in,
    csum,
    ge,
    ga,
    tap_in,
    gain_in,
    gi_in,
    embed_out,
    grad_out,
    pad,
    unit,
    invs,
    normed,
    gb,
    back,
    w_gelu,
    asum,
    tap_sum,
    gain_sum,
    gi_sum,
    go_sum,
    rows_out,
):
    slots, _, side, chans = own.shape
    hidden = w_in.shape[1]
    pixels = side * side
    count, begin, me, mine = meta[0], begin_in[0], meta[2], meta[3]
    for target, source in ((asum, asum_in), (tap_sum, tap_in), (gain_sum, gain_in), (gi_sum, gi_in)):
        target[...] = source[...]
    embed_out[...] = jnp.zeros_like(embed_out)

    split_weights(w_in, w_gelu)
    paired = lax.rem(me, 2) * -2 + 1

    def strip(column, which, slot):
        link = links[column, slot]
        index = lax.rem(jnp.maximum(link, 0), slots)
        aside = lax.div(link, slots) - me
        here, pair, cross = own[index, which], halo_pair[index, which], halo_cross[index, which]
        chosen = jnp.where(aside == 0, here, jnp.where(aside == paired, pair, cross)).astype(jnp.float32)
        return jnp.where(link >= 0, chosen, 0.0)

    lines = side + 2
    plane = lines * LINE_PITCH
    across = [a * LINE_PITCH + FIRST - 1 + b for a in range(3) for b in range(3)]
    along = [plane + b * LINE_PITCH + FIRST - 1 + a for a in range(3) for b in range(3)]
    far = (side - 1) * LINE_PITCH
    starts = [
        across,
        [start + far for start in across],
        along,
        [start + far for start in along],
    ]

    @pl.loop(0, lax.div(count + BORDER_TILES - 1, BORDER_TILES))
    def _(step):
        for part in range(BORDER_TILES):
            slot = step * BORDER_TILES + part
            rows = part * (pad.shape[0] // BORDER_TILES) + FIRST
            columns = rows + plane
            up, down, left, right = strip(0, 1, slot), strip(1, 0, slot), strip(2, 3, slot), strip(3, 2, slot)
            edge = [own[slot, i].astype(jnp.float32) for i in range(4)]
            deep = [inner[slot, i].astype(jnp.float32) for i in range(4)]
            for at, bodies, head, tail in (
                (rows, (up, edge[0], deep[0], deep[1], edge[1], down), left, right),
                (columns, (left, edge[2], deep[2], deep[3], edge[3], right), up, down),
            ):
                for line, body in zip((0, 1, 2, side - 1, side, side + 1), bodies, strict=True):
                    pad[pl.ds(at + line * LINE_PITCH, side), :] = body
                pad[pl.ds(at + LINE_PITCH - 1, side, stride=LINE_PITCH), :] = head
                pad[pl.ds(at + LINE_PITCH + side, side, stride=LINE_PITCH), :] = tail
            last = (side + 1) * LINE_PITCH
            for corner, in_rows, in_columns in (
                (strip(4, 1, slot)[side - 1 :], -1, -1),
                (strip(5, 1, slot)[:1], side, last - 1),
                (strip(6, 0, slot)[side - 1 :], last - 1, side),
                (strip(7, 0, slot)[:1], last + side, last + side),
            ):
                pad[pl.ds(rows + in_rows, 1), :] = corner
                pad[pl.ds(columns + in_columns, 1), :] = corner
        run_lines(
            step,
            BORDER_TILES,
            starts,
            [False, False, True, True],
            (kern, gain[...], w_gelu, w_in_t),
            (pad, unit, invs, normed, gb, back),
            (asum, ga, tap_sum, gain_sum, gi_sum),
        )

    asum[...] = 0.7071067811865476 * asum[...]
    go_sum[...] = lax.dot_general(
        asum[...], ge[...], (((0,), (0,)), ((), ())), precision=HIGHEST, preferred_element_type=jnp.float32
    )
    projected = jnp.dot(
        asum[...], w_out[...].astype(jnp.float32), precision=HIGHEST, preferred_element_type=jnp.float32
    )
    rows_out[...] = (csum[...] + projected) * (1.0 / pixels)

    @pl.loop(0, count)
    def _(slot):
        rank = lax.rem(begin + slot, peers * work)
        block = dealing[lax.rem(rank, peers)] ^ me
        embed_out[pl.ds(block * work + lax.div(rank, peers), 1), :] = rows_out[pl.ds(slot, 1), :]

    per = hidden // parts
    for block in range(parts):
        to = block ^ mine
        columns, offset = divmod(block * per, chans)
        grad_out[to, :per, :] = gi_sum[offset : offset + per, columns * chans : (columns + 1) * chans]
        grad_out[to, per : 2 * per, :] = go_sum[block * per : (block + 1) * per, :]
        grad_out[to, 2 * per :, :] = jnp.zeros((SMALL_ROWS, chans), jnp.float32)
    half = side // 2
    for i in range(9):
        grad_out[(i // SMALL_ROWS) ^ mine, pl.ds(2 * per + i % SMALL_ROWS, 1), :] = math.sqrt(chans) * jnp.sum(
            tap_sum[i * half : (i + 1) * half, :], axis=0, keepdims=True
        )
    grad_out[1 ^ mine, pl.ds(2 * per + 1, 1), :] = math.sqrt(chans) * (
        jnp.sum(gain_sum[...], axis=0, keepdims=True) / gain[...]
    )


def unpack_kernel(parts, meta, near, far, gk, gg, gi, go, packed):
    mine = meta[3]
    packed[: parts // 2] = near[...]
    packed[parts // 2 :] = far[...]
    hidden, chans = go.shape
    per = hidden // parts
    for block in range(parts):
        at = block ^ mine
        columns, offset = divmod(block * per, chans)
        gi[offset : offset + per, columns * chans : (columns + 1) * chans] = packed[at, :per, :]
        go[block * per : (block + 1) * per, :] = packed[at, per : 2 * per, :]
    gk[:SMALL_ROWS, :] = packed[mine, 2 * per :, :]
    gk[SMALL_ROWS:9, :] = packed[1 ^ mine, 2 * per : 2 * per + 1, :]
    gg[...] = packed[1 ^ mine, 2 * per + 1 : 2 * per + 2, :]


def local(features, tissue_count, neighbors, worker_perm, rotation, kernel, gain, w_in, w_out, cotangent):
    feats = features[0]
    slots, side, _, chans = feats.shape
    hidden = w_in.shape[1]
    cot_rows = cotangent[0]
    work = cot_rows.shape[0]
    peers = lax.axis_size("tile")
    slides = lax.axis_size("slide")
    me = lax.axis_index("tile")
    slide_bits, tile_bits = bits_of(slides), bits_of(peers)
    halving = [("slide", bit) for bit in slide_bits] + [("tile", tile_bits[0])]
    parts = 1 << len(halving)
    mine = jnp.zeros((), jnp.int32)
    for place, (axis, bit) in enumerate(reversed(halving)):
        mine = mine + jnp.where((lax.axis_index(axis) & bit) > 0, 1 << place, 0)

    strips, inner, csum = border_strips(feats)
    gathered = jnp.concatenate(
        [cot_rows, jnp.broadcast_to(tissue_count.astype(jnp.float32), (8, chans))], axis=0
    )[None]
    for bit in tile_bits:
        arrived = swap(gathered, "tile", bit)
        if bit == tile_bits[0]:
            halo_pair = swap(strips, "tile", 1)
            arrived, strips = lax.optimization_barrier((arrived, strips))
        if bit < tile_bits[-1]:
            gathered = jnp.concatenate([gathered, arrived], axis=0)
    arrived, strips = lax.optimization_barrier((arrived, strips))
    cross = [(i, i + 1) for i in range(1, peers - 1, 2)]
    halo_cross = lax.ppermute(strips, "tile", cross + [(j, i) for i, j in cross])
    meta = jnp.stack([tissue_count[0, 0], rotation[0], me, mine]).astype(jnp.int32)

    f32 = jnp.float32
    vmem = pl.BlockSpec(memory_space=pltpu.VMEM)
    smem = pl.BlockSpec(memory_space=pltpu.SMEM)
    shape = jax.ShapeDtypeStruct
    params = pltpu.CompilerParams(vmem_limit_bytes=VMEM_BYTES)
    inner_params = pltpu.CompilerParams(vmem_limit_bytes=INNER_BYTES)
    gains = gain[None]
    per = hidden // parts
    block_rows = 2 * per + SMALL_ROWS

    far_space = pl.BlockSpec(memory_space=pltpu.HBM)
    near_rows = peers // 2 * (work + 8)
    asum, ge, ga, tap_sum, gain_sum, gi_sum, w_in_t, begin = pl.pallas_call(
        functools.partial(inner_kernel, peers, work),
        in_specs=[smem] * 2 + [far_space] + [vmem] * 5 + [far_space],
        out_specs=[vmem] * 7 + [smem],
        out_shape=[
            shape((slots, hidden), f32),
            shape((slots, chans), f32),
            shape((slots, hidden), f32),
            shape((9 * (side // 2), chans), f32),
            shape((side // 2, chans), f32),
            shape((chans, hidden), f32),
            shape((hidden, chans), jnp.bfloat16),
            shape((1,), jnp.int32),
        ],
        scratch_shapes=line_scratch(INNER_TILES, (side + 1) * INNER_PITCH, side - 2, side, chans, hidden)
        + [
            pltpu.VMEM(feats.shape, jnp.bfloat16),
            pltpu.VMEM((hidden, chans), jnp.bfloat16),
            pltpu.VMEM((2 * near_rows, chans), f32),
            pltpu.SemaphoreType.DMA((slots // INNER_TILES,)),
            pltpu.SemaphoreType.DMA,
        ],
        compiler_params=inner_params,
    )(
        meta,
        worker_perm[0],
        feats,
        gathered.reshape(near_rows, chans),
        arrived.reshape(near_rows, chans),
        kernel,
        gains,
        w_in,
        w_out,
    )
    embeds, packed = pl.pallas_call(
        functools.partial(border_kernel, peers, work, parts),
        in_specs=[smem] * 4 + [vmem] * 16,
        out_specs=[vmem] * 2,
        out_shape=[shape((peers * work, chans), f32), shape((parts, block_rows, chans), f32)],
        scratch_shapes=line_scratch(BORDER_TILES, 2 * (side + 2) * LINE_PITCH, 4, side, chans, hidden)
        + [
            pltpu.VMEM((slots, hidden), f32),
            pltpu.VMEM((9 * (side // 2), chans), f32),
            pltpu.VMEM((side // 2, chans), f32),
            pltpu.VMEM((chans, hidden), f32),
            pltpu.VMEM((hidden, chans), f32),
            pltpu.VMEM((slots, chans), f32),
        ],
        compiler_params=params,
    )(
        meta,
        begin,
        worker_perm[0],
        neighbors[0].T,
        strips,
        inner,
        halo_pair,
        halo_cross,
        kernel,
        gains,
        w_in,
        w_in_t,
        w_out,
        asum,
        csum,
        ge,
        ga,
        tap_sum,
        gain_sum,
        gi_sum,
    )

    held = packed
    for axis, bit in halving[:-1]:
        half = held.shape[0] // 2
        held = held[:half] + swap(held[half:], axis, bit)
    embeds = embeds.reshape(peers, work, chans)
    for place, bit in enumerate(tile_bits):
        paired = embeds.reshape(embeds.shape[0] // 2, 2, work, chans)
        keep, send = paired[:, 0], paired[:, 1]
        if place == 0:
            mine_part, other_part = held[0], held[1]
        else:
            mine_part, other_part = held, held
        outgoing = jnp.concatenate([send.reshape(-1, chans), other_part], axis=0)
        incoming = swap(outgoing, "tile", bit)
        rows = send.shape[0] * work
        embeds = keep + incoming[:rows].reshape(keep.shape)
        held = mine_part + incoming[rows:]
    held = held[None]
    for axis, bit in reversed(halving[1:]):
        held = jnp.concatenate([held, swap(held, axis, bit)], axis=0)
    far = swap(held, *halving[0])
    gk, gg, gi, go = pl.pallas_call(
        functools.partial(unpack_kernel, parts),
        in_specs=[smem, vmem, vmem],
        out_specs=[vmem] * 4,
        out_shape=[
            jax.ShapeDtypeStruct((9, chans), f32),
            jax.ShapeDtypeStruct((1, chans), f32),
            jax.ShapeDtypeStruct((chans, hidden), f32),
            jax.ShapeDtypeStruct((hidden, chans), f32),
        ],
        scratch_shapes=[pltpu.VMEM((parts, block_rows, chans), f32)],
        compiler_params=params,
    )(meta, held, far)
    return embeds, gk, gg[0], gi, go


def solution(mesh):
    placed = (
        P("slide", "tile", None, None, None),
        P("slide", "tile"),
        P("slide", "tile", None),
        P("slide", None),
        P("slide"),
        P(),
        P(),
        P(),
        P(),
        P("slide", "tile", None),
    )
    return jax.shard_map(
        local,
        mesh=mesh,
        in_specs=placed,
        out_specs=(P("slide", "tile", None), P(), P(), P(), P()),
        check_vma=False,
    )
```

```python
import functools
import math

import jax
import jax.numpy as jnp
from jax import lax
from jax.experimental import pallas as pl
from jax.experimental.pallas import tpu as pltpu
from jax.sharding import PartitionSpec as P

HIGHEST = lax.Precision.HIGHEST
FIRST = 8
INNER_PITCH = 24
LINE_PITCH = 32
INNER_TILES = 4
BORDER_TILES = 16
SMALL_ROWS = 8
STRIP_TILES = 8
VMEM_BYTES = 32 * 1024 * 1024
STRIP_BYTES = 49 * 1024 * 1024
INNER_BYTES = 48 * 1024 * 1024


def bits_of(count):
    return [1 << bit for bit in range(count.bit_length() - 1)]


def swap(value, axis, bit):
    count = lax.axis_size(axis)
    return lax.ppermute(value, axis, [(i, i ^ bit) for i in range(count)])


def strip_kernel(tiles_hbm, strips, inner, csum, tiles, sems):
    slots, side, _, chans = tiles_hbm.shape
    columns = (0, side - 1, 1, side - 2)
    rows = (len(columns) + 1) * side
    row = lax.broadcasted_iota(jnp.int32, (rows, side * side), 0)
    pixel = lax.broadcasted_iota(jnp.int32, (rows, side * side), 1)
    group = lax.div(row, side)
    column = jnp.where(group == 0, columns[0], jnp.where(group == 1, columns[1], jnp.where(group == 2, columns[2], columns[3])))
    picked = (pixel == (row - group * side) * side + column) | (group == len(columns))
    select = jnp.where(picked, 1.0, 0.0).astype(jnp.bfloat16)

    def tiles_copy(step):
        taken = pl.ds(step * STRIP_TILES, STRIP_TILES)
        return pltpu.make_async_copy(tiles_hbm.at[taken], tiles.at[taken], sems.at[step])

    @pl.loop(0, slots // STRIP_TILES)
    def _(step):
        tiles_copy(step).start()

    @pl.loop(0, slots // STRIP_TILES)
    def _(step):
        tiles_copy(step).wait()
        for part in range(STRIP_TILES):
            slot = step * STRIP_TILES + part
            tile = tiles[slot].reshape(side * side, chans)
            found = jnp.dot(select, tile, preferred_element_type=jnp.float32)
            lines = found[: len(columns) * side].astype(jnp.bfloat16)
            strips[slot, 0] = tiles[slot, 0]
            strips[slot, 1] = tiles[slot, side - 1]
            strips[slot, 2] = lines[:side]
            strips[slot, 3] = lines[side : 2 * side]
            inner[slot, 0] = tiles[slot, 1]
            inner[slot, 1] = tiles[slot, side - 2]
            inner[slot, 2] = lines[2 * side : 3 * side]
            inner[slot, 3] = lines[3 * side :]
            csum[pl.ds(slot, 1), :] = found[len(columns) * side : len(columns) * side + 1]


def border_strips(tiles):
    slots, side, _, chans = tiles.shape
    shape = jax.ShapeDtypeStruct((slots, 4, side, chans), jnp.bfloat16)
    spec = pl.BlockSpec(memory_space=pltpu.VMEM)
    return pl.pallas_call(
        strip_kernel,
        in_specs=[pl.BlockSpec(memory_space=pltpu.HBM)],
        out_specs=[spec] * 3,
        out_shape=[shape, shape, jax.ShapeDtypeStruct((slots, chans), jnp.float32)],
        scratch_shapes=[
            pltpu.VMEM(tiles.shape, jnp.bfloat16),
            pltpu.SemaphoreType.DMA((slots // STRIP_TILES,)),
        ],
        compiler_params=pltpu.CompilerParams(vmem_limit_bytes=STRIP_BYTES),
    )(tiles)


def spread(rows, lines):
    return rows.reshape(lines, rows.shape[0] // lines, rows.shape[1])


def run_lines(
    step, tiles, starts, masked, weights, state, sums
):
    kern, gains, w_gelu, w_in_t = weights
    pad, unit, invs, normed, gb, back = state
    asum, ga, tap_sum, gain_sum, gi_sum = sums
    lines = len(starts)
    pad_rows = pad.shape[0] // tiles
    pixels = normed.shape[0] // tiles
    side = pixels // lines
    hidden, chans = w_in_t.shape
    half = side // 2
    gains_root = gains * math.sqrt(chans)
    wide_taps = kern[...].astype(jnp.float32)
    taps = [jnp.broadcast_to(wide_taps[i : i + 1, :], (side, chans)) for i in range(9)]
    place = lax.broadcasted_iota(jnp.int32, (side, hidden), 0)
    inside = jnp.where((place > 0) & (place < side - 1), 1.0, 0.0)
    for part in range(tiles):
        base = part * pad_rows
        for line in range(lines):
            depth = None
            for tap in range(9):
                term = pad[pl.ds(base + starts[line][tap], side), :] * taps[tap]
                depth = term if depth is None else depth + term
            centered = depth - jnp.mean(depth, axis=1, keepdims=True)
            inverse = lax.rsqrt(jnp.sum(centered * centered, axis=1, keepdims=True) + chans * 1e-06)
            units = centered * inverse
            at = part * pixels + line * side
            unit[at : at + side, :] = units
            invs[at : at + side, :] = jnp.broadcast_to(inverse, (side, chans))
            normed[at : at + side, :] = (units * gains_root).astype(jnp.bfloat16)
    for part in range(tiles):
        slot = step * tiles + part
        rows = slice(part * pixels, (part + 1) * pixels)
        doubled = jnp.concatenate([normed[rows, :]] * 2, axis=1)
        scaled = jnp.dot(doubled, w_gelu[...], preferred_element_type=jnp.float32)
        twice = 1.0 + lax.erf(scaled)
        bell = jnp.exp2(scaled * scaled * -1.4426950408889634)
        act = spread(scaled * twice, lines)
        slope = spread(twice + (scaled * 1.1283791670955126) * bell, lines)
        factor = jnp.broadcast_to(ga[pl.ds(slot, 1), :], (side, hidden))
        factor_inside = factor * inside
        whole = [act[line] for line in range(lines) if not masked[line]]
        partial = [act[line] for line in range(lines) if masked[line]]
        total = functools.reduce(jnp.add, partial) * inside
        if whole:
            total = total + functools.reduce(jnp.add, whole)
        asum[pl.ds(slot, 1), :] += jnp.sum(total, axis=0, keepdims=True)
        for line in range(lines):
            at = part * pixels + line * side
            gb[at : at + side, :] = (slope[line] * (factor_inside if masked[line] else factor)).astype(jnp.bfloat16)
    back[...] = jnp.dot(gb[...], w_in_t[...], preferred_element_type=jnp.float32)
    gi_sum[...] += lax.dot_general(normed[...], gb[...], (((0,), (0,)), ((), ())), preferred_element_type=jnp.float32)
    gain_part = jnp.zeros((half, chans), jnp.float32)
    tap_part = [jnp.zeros((half, chans), jnp.float32) for _ in range(9)]
    for part in range(tiles):
        base = part * pad_rows
        for line in range(lines):
            at = part * pixels + line * side
            units = unit[at : at + side, :]
            grad_unit = back[at : at + side, :] * gains
            product = grad_unit * units
            gain_part = gain_part + (product[:half] + product[half:])
            grad_depth = invs[at : at + side, :] * (
                grad_unit
                - jnp.mean(grad_unit, axis=1, keepdims=True)
                - units * jnp.sum(product, axis=1, keepdims=True)
            )
            for tap in range(9):
                term = grad_depth * pad[pl.ds(base + starts[line][tap], side), :]
                tap_part[tap] = tap_part[tap] + (term[:half] + term[half:])
    gain_sum[...] += gain_part
    for tap in range(9):
        tap_sum[tap * half : (tap + 1) * half, :] += tap_part[tap]


def line_scratch(tiles, pad_rows, lines, side, chans, hidden):
    f32, bf16 = jnp.float32, jnp.bfloat16
    pixels = tiles * lines * side
    return [
        pltpu.VMEM((tiles * pad_rows, chans), f32),
        pltpu.VMEM((pixels, chans), f32),
        pltpu.VMEM((pixels, chans), f32),
        pltpu.VMEM((pixels, chans), bf16),
        pltpu.VMEM((pixels, hidden), bf16),
        pltpu.VMEM((pixels, chans), f32),
        pltpu.VMEM((2 * chans, hidden), bf16),
    ]


def split_weights(w_in, w_gelu):
    chans = w_in.shape[0]
    scaled = w_in[...].astype(jnp.float32) * 0.7071067811865476
    high = scaled.astype(jnp.bfloat16)
    w_gelu[:chans, :] = high
    w_gelu[chans:, :] = (scaled - high.astype(jnp.float32)).astype(jnp.bfloat16)


def inner_kernel(
    peers,
    work,
    meta,
    dealing,
    feats_hbm,
    cot_near,
    cot_far,
    kern,
    gain,
    w_in,
    w_out_hbm,
    asum,
    ge,
    ga,
    tap_sum,
    gain_sum,
    gi_sum,
    w_in_t,
    begin_out,
    pad,
    unit,
    invs,
    normed,
    gb,
    back,
    w_gelu,
    feats,
    w_out,
    cot_all,
    tile_sems,
    weight_sem,
):
    side = feats.shape[1]
    chans = feats.shape[3]
    pixels = side * side
    cot_rows = cot_all.shape[0] // peers
    count, turned, me = meta[0], meta[1], meta[2]
    steps = lax.div(count + INNER_TILES - 1, INNER_TILES)

    def tiles_copy(step):
        taken = pl.ds(step * INNER_TILES, INNER_TILES)
        return pltpu.make_async_copy(feats_hbm.at[taken], feats.at[taken], tile_sems.at[step])

    weight_copy = pltpu.make_async_copy(w_out_hbm, w_out, weight_sem)
    weight_copy.start()

    @pl.loop(0, steps)
    def _(step):
        tiles_copy(step).start()

    half_rows = cot_near.shape[0]
    cot_all[:half_rows, :] = cot_near[...]
    cot_all[half_rows:, :] = cot_far[...]
    counts = cot_all[pl.ds(work, peers, stride=cot_rows), :]
    whose = lax.broadcasted_iota(jnp.int32, counts.shape, 0) ^ me
    lane = lax.broadcasted_iota(jnp.int32, counts.shape, 1)
    begin = turned + jnp.sum(jnp.where((whose < me) & (lane == 0), counts, 0.0)).astype(jnp.int32)
    begin_out[0] = begin
    split_weights(w_in, w_gelu)
    for ref in (asum, ge, tap_sum, gain_sum, gi_sum, pad):
        ref[...] = jnp.zeros_like(ref)

    @pl.loop(0, count)
    def _(slot):
        rank = lax.rem(begin + slot, peers * work)
        block = dealing[lax.rem(rank, peers)] ^ me
        row = block * cot_rows + lax.div(rank, peers)
        ge[pl.ds(slot, 1), :] = cot_all[pl.ds(row, 1), :] * (1.0 / pixels)

    w_in_t[...] = w_in[...].astype(jnp.float32).T.astype(jnp.bfloat16)
    weight_copy.wait()
    ga[...] = 0.5 * lax.dot_general(
        ge[...],
        w_out[...].astype(jnp.float32),
        (((1,), (1,)), ((), ())),
        precision=HIGHEST,
        preferred_element_type=jnp.float32,
    )
    starts = [
        [(y - 1 + a) * INNER_PITCH + FIRST - 1 + b for a in range(3) for b in range(3)] for y in range(1, side - 1)
    ]

    @pl.loop(0, steps)
    def _(step):
        tiles_copy(step).wait()
        for part in range(INNER_TILES):
            slot = step * INNER_TILES + part
            base = part * (pad.shape[0] // INNER_TILES)
            for y in range(side):
                pad[pl.ds(base + y * INNER_PITCH + FIRST, side), :] = feats[slot, y].astype(jnp.float32)
        run_lines(
            step,
            INNER_TILES,
            starts,
            [True] * len(starts),
            (kern, gain[...], w_gelu, w_in_t),
            (pad, unit, invs, normed, gb, back),
            (asum, ga, tap_sum, gain_sum, gi_sum),
        )


def border_kernel(
    peers,
    work,
    parts,
    meta,
    begin_in,
    dealing,
    links,
    own,
    inner,
    halo_pair,
    halo_cross,
    kern,
    gain,
    w_in,
    w_in_t,
    w_out,
    asum_in,
    csum,
    ge,
    ga,
    tap_in,
    gain_in,
    gi_in,
    embed_out,
    grad_out,
    pad,
    unit,
    invs,
    normed,
    gb,
    back,
    w_gelu,
    asum,
    tap_sum,
    gain_sum,
    gi_sum,
    go_sum,
    rows_out,
):
    slots, _, side, chans = own.shape
    hidden = w_in.shape[1]
    pixels = side * side
    count, begin, me, mine = meta[0], begin_in[0], meta[2], meta[3]
    for target, source in ((asum, asum_in), (tap_sum, tap_in), (gain_sum, gain_in), (gi_sum, gi_in)):
        target[...] = source[...]
    embed_out[...] = jnp.zeros_like(embed_out)

    split_weights(w_in, w_gelu)
    paired = lax.rem(me, 2) * -2 + 1

    def strip(column, which, slot):
        link = links[column, slot]
        index = lax.rem(jnp.maximum(link, 0), slots)
        aside = lax.div(link, slots) - me
        here, pair, cross = own[index, which], halo_pair[index, which], halo_cross[index, which]
        chosen = jnp.where(aside == 0, here, jnp.where(aside == paired, pair, cross)).astype(jnp.float32)
        return jnp.where(link >= 0, chosen, 0.0)

    lines = side + 2
    plane = lines * LINE_PITCH
    across = [a * LINE_PITCH + FIRST - 1 + b for a in range(3) for b in range(3)]
    along = [plane + b * LINE_PITCH + FIRST - 1 + a for a in range(3) for b in range(3)]
    far = (side - 1) * LINE_PITCH
    starts = [
        across,
        [start + far for start in across],
        along,
        [start + far for start in along],
    ]

    @pl.loop(0, lax.div(count + BORDER_TILES - 1, BORDER_TILES))
    def _(step):
        for part in range(BORDER_TILES):
            slot = step * BORDER_TILES + part
            rows = part * (pad.shape[0] // BORDER_TILES) + FIRST
            columns = rows + plane
            up, down, left, right = strip(0, 1, slot), strip(1, 0, slot), strip(2, 3, slot), strip(3, 2, slot)
            edge = [own[slot, i].astype(jnp.float32) for i in range(4)]
            deep = [inner[slot, i].astype(jnp.float32) for i in range(4)]
            for at, bodies, head, tail in (
                (rows, (up, edge[0], deep[0], deep[1], edge[1], down), left, right),
                (columns, (left, edge[2], deep[2], deep[3], edge[3], right), up, down),
            ):
                for line, body in zip((0, 1, 2, side - 1, side, side + 1), bodies, strict=True):
                    pad[pl.ds(at + line * LINE_PITCH, side), :] = body
                pad[pl.ds(at + LINE_PITCH - 1, side, stride=LINE_PITCH), :] = head
                pad[pl.ds(at + LINE_PITCH + side, side, stride=LINE_PITCH), :] = tail
            last = (side + 1) * LINE_PITCH
            for corner, in_rows, in_columns in (
                (strip(4, 1, slot)[side - 1 :], -1, -1),
                (strip(5, 1, slot)[:1], side, last - 1),
                (strip(6, 0, slot)[side - 1 :], last - 1, side),
                (strip(7, 0, slot)[:1], last + side, last + side),
            ):
                pad[pl.ds(rows + in_rows, 1), :] = corner
                pad[pl.ds(columns + in_columns, 1), :] = corner
        run_lines(
            step,
            BORDER_TILES,
            starts,
            [False, False, True, True],
            (kern, gain[...], w_gelu, w_in_t),
            (pad, unit, invs, normed, gb, back),
            (asum, ga, tap_sum, gain_sum, gi_sum),
        )

    asum[...] = 0.7071067811865476 * asum[...]
    go_sum[...] = lax.dot_general(
        asum[...], ge[...], (((0,), (0,)), ((), ())), precision=HIGHEST, preferred_element_type=jnp.float32
    )
    projected = jnp.dot(
        asum[...], w_out[...].astype(jnp.float32), precision=HIGHEST, preferred_element_type=jnp.float32
    )
    rows_out[...] = (csum[...] + projected) * (1.0 / pixels)

    @pl.loop(0, count)
    def _(slot):
        rank = lax.rem(begin + slot, peers * work)
        block = dealing[lax.rem(rank, peers)] ^ me
        embed_out[pl.ds(block * work + lax.div(rank, peers), 1), :] = rows_out[pl.ds(slot, 1), :]

    per = hidden // parts
    for block in range(parts):
        to = block ^ mine
        columns, offset = divmod(block * per, chans)
        grad_out[to, :per, :] = gi_sum[offset : offset + per, columns * chans : (columns + 1) * chans]
        grad_out[to, per : 2 * per, :] = go_sum[block * per : (block + 1) * per, :]
        grad_out[to, 2 * per :, :] = jnp.zeros((SMALL_ROWS, chans), jnp.float32)
    half = side // 2
    for i in range(9):
        grad_out[(i // SMALL_ROWS) ^ mine, pl.ds(2 * per + i % SMALL_ROWS, 1), :] = math.sqrt(chans) * jnp.sum(
            tap_sum[i * half : (i + 1) * half, :], axis=0, keepdims=True
        )
    grad_out[1 ^ mine, pl.ds(2 * per + 1, 1), :] = math.sqrt(chans) * (
        jnp.sum(gain_sum[...], axis=0, keepdims=True) / gain[...]
    )


def unpack_kernel(parts, meta, near, far, gk, gg, gi, go, packed):
    mine = meta[3]
    packed[: parts // 2] = near[...]
    packed[parts // 2 :] = far[...]
    hidden, chans = go.shape
    per = hidden // parts
    for block in range(parts):
        at = block ^ mine
        columns, offset = divmod(block * per, chans)
        gi[offset : offset + per, columns * chans : (columns + 1) * chans] = packed[at, :per, :]
        go[block * per : (block + 1) * per, :] = packed[at, per : 2 * per, :]
    gk[:SMALL_ROWS, :] = packed[mine, 2 * per :, :]
    gk[SMALL_ROWS:9, :] = packed[1 ^ mine, 2 * per : 2 * per + 1, :]
    gg[...] = packed[1 ^ mine, 2 * per + 1 : 2 * per + 2, :]


def local(features, tissue_count, neighbors, worker_perm, rotation, kernel, gain, w_in, w_out, cotangent):
    feats = features[0]
    slots, side, _, chans = feats.shape
    hidden = w_in.shape[1]
    cot_rows = cotangent[0]
    work = cot_rows.shape[0]
    peers = lax.axis_size("tile")
    slides = lax.axis_size("slide")
    me = lax.axis_index("tile")
    slide_bits, tile_bits = bits_of(slides), bits_of(peers)
    halving = [("slide", bit) for bit in slide_bits] + [("tile", tile_bits[0])]
    parts = 1 << len(halving)
    mine = jnp.zeros((), jnp.int32)
    for place, (axis, bit) in enumerate(reversed(halving)):
        mine = mine + jnp.where((lax.axis_index(axis) & bit) > 0, 1 << place, 0)

    strips, inner, csum = border_strips(feats)
    gathered = jnp.concatenate(
        [cot_rows, jnp.broadcast_to(tissue_count.astype(jnp.float32), (8, chans))], axis=0
    )[None]
    for bit in tile_bits:
        arrived = swap(gathered, "tile", bit)
        if bit == tile_bits[0]:
            halo_pair = swap(strips, "tile", 1)
            arrived, strips = lax.optimization_barrier((arrived, strips))
        if bit < tile_bits[-1]:
            gathered = jnp.concatenate([gathered, arrived], axis=0)
    arrived, strips = lax.optimization_barrier((arrived, strips))
    cross = [(i, i + 1) for i in range(1, peers - 1, 2)]
    halo_cross = lax.ppermute(strips, "tile", cross + [(j, i) for i, j in cross])
    meta = jnp.stack([tissue_count[0, 0], rotation[0], me, mine]).astype(jnp.int32)

    f32 = jnp.float32
    vmem = pl.BlockSpec(memory_space=pltpu.VMEM)
    smem = pl.BlockSpec(memory_space=pltpu.SMEM)
    shape = jax.ShapeDtypeStruct
    params = pltpu.CompilerParams(vmem_limit_bytes=VMEM_BYTES)
    inner_params = pltpu.CompilerParams(vmem_limit_bytes=INNER_BYTES)
    gains = gain[None]
    per = hidden // parts
    block_rows = 2 * per + SMALL_ROWS

    far_space = pl.BlockSpec(memory_space=pltpu.HBM)
    near_rows = peers // 2 * (work + 8)
    asum, ge, ga, tap_sum, gain_sum, gi_sum, w_in_t, begin = pl.pallas_call(
        functools.partial(inner_kernel, peers, work),
        in_specs=[smem] * 2 + [far_space] + [vmem] * 5 + [far_space],
        out_specs=[vmem] * 7 + [smem],
        out_shape=[
            shape((slots, hidden), f32),
            shape((slots, chans), f32),
            shape((slots, hidden), f32),
            shape((9 * (side // 2), chans), f32),
            shape((side // 2, chans), f32),
            shape((chans, hidden), f32),
            shape((hidden, chans), jnp.bfloat16),
            shape((1,), jnp.int32),
        ],
        scratch_shapes=line_scratch(INNER_TILES, (side + 1) * INNER_PITCH, side - 2, side, chans, hidden)
        + [
            pltpu.VMEM(feats.shape, jnp.bfloat16),
            pltpu.VMEM((hidden, chans), jnp.bfloat16),
            pltpu.VMEM((2 * near_rows, chans), f32),
            pltpu.SemaphoreType.DMA((slots // INNER_TILES,)),
            pltpu.SemaphoreType.DMA,
        ],
        compiler_params=inner_params,
    )(
        meta,
        worker_perm[0],
        feats,
        gathered.reshape(near_rows, chans),
        arrived.reshape(near_rows, chans),
        kernel,
        gains,
        w_in,
        w_out,
    )
    embeds, packed = pl.pallas_call(
        functools.partial(border_kernel, peers, work, parts),
        in_specs=[smem] * 4 + [vmem] * 16,
        out_specs=[vmem] * 2,
        out_shape=[shape((peers * work, chans), f32), shape((parts, block_rows, chans), f32)],
        scratch_shapes=line_scratch(BORDER_TILES, 2 * (side + 2) * LINE_PITCH, 4, side, chans, hidden)
        + [
            pltpu.VMEM((slots, hidden), f32),
            pltpu.VMEM((9 * (side // 2), chans), f32),
            pltpu.VMEM((side // 2, chans), f32),
            pltpu.VMEM((chans, hidden), f32),
            pltpu.VMEM((hidden, chans), f32),
            pltpu.VMEM((slots, chans), f32),
        ],
        compiler_params=params,
    )(
        meta,
        begin,
        worker_perm[0],
        neighbors[0].T,
        strips,
        inner,
        halo_pair,
        halo_cross,
        kernel,
        gains,
        w_in,
        w_in_t,
        w_out,
        asum,
        csum,
        ge,
        ga,
        tap_sum,
        gain_sum,
        gi_sum,
    )

    held = packed
    for axis, bit in halving[:-1]:
        half = held.shape[0] // 2
        held = held[:half] + swap(held[half:], axis, bit)
    embeds = embeds.reshape(peers, work, chans)
    for place, bit in enumerate(tile_bits):
        paired = embeds.reshape(embeds.shape[0] // 2, 2, work, chans)
        keep, send = paired[:, 0], paired[:, 1]
        if place == 0:
            mine_part, other_part = held[0], held[1]
        else:
            mine_part, other_part = held, held
        outgoing = jnp.concatenate([send.reshape(-1, chans), other_part], axis=0)
        incoming = swap(outgoing, "tile", bit)
        rows = send.shape[0] * work
        embeds = keep + incoming[:rows].reshape(keep.shape)
        held = mine_part + incoming[rows:]
    held = held[None]
    for axis, bit in reversed(halving[1:]):
        held = jnp.concatenate([held, swap(held, axis, bit)], axis=0)
    far = swap(held, *halving[0])
    gk, gg, gi, go = pl.pallas_call(
        functools.partial(unpack_kernel, parts),
        in_specs=[smem, vmem, vmem],
        out_specs=[vmem] * 4,
        out_shape=[
            jax.ShapeDtypeStruct((9, chans), f32),
            jax.ShapeDtypeStruct((1, chans), f32),
            jax.ShapeDtypeStruct((chans, hidden), f32),
            jax.ShapeDtypeStruct((hidden, chans), f32),
        ],
        scratch_shapes=[pltpu.VMEM((parts, block_rows, chans), f32)],
        compiler_params=params,
    )(meta, held, far)
    return embeds, gk, gg[0], gi, go


def solution(mesh):
    placed = (
        P("slide", "tile", None, None, None),
        P("slide", "tile"),
        P("slide", "tile", None),
        P("slide", None),
        P("slide"),
        P(),
        P(),
        P(),
        P(),
        P("slide", "tile", None),
    )
    return jax.shard_map(
        local,
        mesh=mesh,
        in_specs=placed,
        out_specs=(P("slide", "tile", None), P(), P(), P(), P()),
        check_vma=False,
    )
```
